512 devices in a mesh: own: 128 (over y, z, core), rep: 4 (over x).
Axes of the slice: x: 4, y: 8, z: 8, core: 2. Of those that a mesh axis runs over, the one named last changes fastest.
Arguments:
- sample_grads: bfloat16 [131072, 1024], P(('own', 'rep')), may hold values from -6 to 6
- send_count: int32 [512, 128], P(('own', 'rep')), may hold values from 1 to 4, as said below
- send_user: int32 [65536, 4], P(('own', 'rep')), may hold values from 0 to 1
- histories: bfloat16 [1024, 256, 1024], P(('own', 'rep')), may hold values from -6 to 6
- hist_len: int32 [1024], P(('own', 'rep')), may hold values from 64 to 256, as said below
- w_in: bfloat16 [1024, 512], replicated, may hold values from -0.1875 to 0.1875
- w_out: bfloat16 [128, 1024], replicated, may hold values from -0.5 to 0.5
Outputs:
- hist_grad: bfloat16 [1024, 256, 1024], P(('own', 'rep'))
- grad_in: float32 [1024, 512], P(('own', 'rep'))
- grad_out: float32 [128, 1024], P(None, ('own', 'rep'))
The draws below stay inside these ranges and needn't reach their ends.
Inputs may be any that keep to these rules, and one draw needn't show every extreme that they name: `send_count`: within every replica group one owner, drawn anew, receives exactly 4 samples from every device; every other count lies between 1 and 1; a row sums to at most 256. `send_user`: entries at positions c >= the matching send_count are unused. `hist_len`: every device holds one history of length exactly 256.
All inputs are finite; a program needn't handle non-finite values.
Results may differ from the reference program's by a relative error of at most 0.017.
Values may be sent and summed in bfloat16 or wider, within the bound.
A program may use at most 64 MiB of HBM per device.

```python
import jax
import jax.numpy as jnp
from jax import lax

D = 1024
HD = 128
L = 256
U_DEV = 2
S_DEV = 256
CAP = 4
OTHER_MOST = 1
USERS = 1024
SAMPLES = 131072
N_OWN = 128
DEVICES = 512


def draw_send_count(key, part):
    key = jax.random.fold_in(key, 11)
    first, second = jax.random.split(key)
    reps = DEVICES // N_OWN
    busiest = jax.random.randint(first, (reps,), 0, N_OWN)
    others = jax.random.randint(second, (DEVICES, N_OWN), 1, OTHER_MOST + 1)
    group = jnp.arange(DEVICES) % reps
    owner = jnp.arange(N_OWN)
    return jnp.where(owner[None, :] == busiest[group][:, None], CAP, others).astype(jnp.int32)


def draw_hist_len(key, part):
    key = jax.random.fold_in(key, 23)
    first, second = jax.random.split(key)
    base = jax.random.randint(first, (DEVICES * U_DEV,), L // 4, L + 1)
    chosen = jax.random.randint(second, (DEVICES,), 0, U_DEV)
    which = jnp.arange(DEVICES * U_DEV) % U_DEV == jnp.repeat(chosen, U_DEV)
    return jnp.where(which, L, base).astype(jnp.int32)


def with_ends(array, rng, low, largest):
    longest = array.shape.index(max(array.shape))
    spots = []
    for shift in (0, 1):
        where = [jax.random.randint(jax.random.fold_in(rng, axis), (), 0, length) for axis, length in enumerate(array.shape)]
        where[longest] = (where[longest] + shift) % array.shape[longest]
        spots.append(tuple(where))
    return array.at[spots[0]].set(low).at[spots[1]].set(largest)


def levels(own_key, shape, cuts, least, largest):
    def one(dim, shards_of):
        draws = jax.random.uniform(jax.random.fold_in(jax.random.fold_in(own_key, 6), dim), (shards_of,), jnp.float32, least / len(cuts), largest / len(cuts))
        return jnp.repeat(jnp.exp(draws), shape[dim] // shards_of).reshape((-1,) + (1,) * (len(shape) - dim - 1))

    gain = one(*cuts[0])
    for cut in cuts[1:]:
        gain = gain * one(*cut)
    return gain


def normal_values(stream_key, extent, spread, bound, cuts=(), kind=jnp.bfloat16):
    loudness = levels(stream_key, extent, cuts, -0.22, 0.18) if cuts else 1.0
    entries = jax.random.normal(stream_key, extent, jnp.float32) * spread * loudness
    return jnp.minimum(jnp.maximum(entries, -bound), bound).astype(kind)


def setup_inputs(seed: int = 0) -> dict:
    splits = jax.random.split(jax.random.key(seed), 8)
    sample_grads = normal_values(splits[0], (SAMPLES, D), 1.0, 6.0, ((0, 512),))
    send_count = draw_send_count(jax.random.fold_in(splits[7], 71), 0)
    send_user = with_ends(jax.random.randint(splits[2], (DEVICES * N_OWN, CAP), 0, U_DEV), jax.random.fold_in(splits[2], 1), 0, U_DEV - 1).astype(jnp.int32)
    histories = normal_values(splits[3], (USERS, L, D), 1.0, 6.0, ((0, 512),))
    hist_len = draw_hist_len(jax.random.fold_in(splits[7], 71), 0)
    w_in = normal_values(splits[5], (D, 4 * HD), D ** -0.5, 0.1875)
    w_out = normal_values(splits[6], (HD, D), HD ** -0.5, 0.5)
    return {"sample_grads": sample_grads, "send_count": send_count, "send_user": send_user, "histories": histories, "hist_len": hist_len, "w_in": w_in, "w_out": w_out}


def encode(x_f, length, wi_f, wo_f):
    seq = x_f.shape[0]
    width = wo_f.shape[0]
    msq = lax.optimization_barrier(jnp.mean(x_f * x_f, axis=-1, keepdims=True))
    normed = (x_f * lax.rsqrt(msq + 1e-05)).astype(jnp.bfloat16)
    proj = jax.nn.silu(jnp.dot(normed, wi_f.astype(jnp.bfloat16), preferred_element_type=jnp.float32))
    gate_u = proj[:, :width]
    values = proj[:, width:2 * width].astype(jnp.bfloat16)
    query = proj[:, 2 * width:3 * width].astype(jnp.bfloat16)
    keys = proj[:, 3 * width:].astype(jnp.bfloat16)
    scores = jnp.dot(query, keys.T, preferred_element_type=jnp.float32) * width ** (-0.5)
    rowpos = jnp.arange(seq, dtype=jnp.int32)[:, None]
    colpos = jnp.arange(seq, dtype=jnp.int32)[None, :]
    lenf = length.astype(jnp.float32)
    visible = (colpos <= rowpos) & (colpos < length)
    weights = (jnp.where(visible, jax.nn.silu(scores), 0.0) / lenf).astype(jnp.bfloat16)
    attended = jnp.dot(weights, values, preferred_element_type=jnp.float32)
    mixed = (attended * gate_u).astype(jnp.bfloat16)
    out = x_f + jnp.dot(mixed, wo_f.astype(jnp.bfloat16), preferred_element_type=jnp.float32)
    keep = (jnp.arange(seq, dtype=jnp.int32) < length).astype(jnp.float32)
    return lax.optimization_barrier(jnp.sum(out * keep[:, None], axis=0)) / lenf

def user_backward(history, length, grad, wi_f, wo_f):

    def apply(x_f, wi, wo):
        return encode(x_f, length, wi, wo)
    pooled, pull = jax.vjp(apply, history.astype(jnp.float32), wi_f, wo_f)
    dx, dwi, dwo = pull(grad)
    return (dx.astype(jnp.bfloat16), dwi, dwo)

def reference(sample_grads, send_count, send_user, histories, hist_len, w_in, w_out):
    users_total = histories.shape[0]
    width = sample_grads.shape[1]
    reps = DEVICES // N_OWN

    def route(acc, src):
        rows = lax.dynamic_slice_in_dim(sample_grads, src * S_DEV, S_DEV, 0)
        counts = send_count[src]
        slots = lax.dynamic_slice_in_dim(send_user, src * N_OWN, N_OWN, 0)
        offsets = jnp.cumsum(counts) - counts
        position = jnp.arange(CAP, dtype=jnp.int32)
        index = jnp.clip(offsets[:, None] + position[None, :], 0, S_DEV - 1).reshape(-1).astype(jnp.int32)
        live = (position[None, :] < counts[:, None]).reshape(-1)
        picked = jnp.where(live[:, None], rows[index].astype(jnp.float32), 0.0)
        owner = jnp.arange(N_OWN, dtype=jnp.int32)
        target = (((owner * reps + src % reps) * U_DEV)[:, None] + slots).reshape(-1).astype(jnp.int32)
        return (acc + jax.ops.segment_sum(picked, target, num_segments=users_total), None)
    user_grad, unused = lax.scan(route, jnp.zeros((users_total, width), jnp.float32), jnp.arange(DEVICES, dtype=jnp.int32))
    wi_f = w_in.astype(jnp.float32)
    wo_f = w_out.astype(jnp.float32)

    def each_user(carry, item):
        history, length, grad = item
        dx, dwi, dwo = user_backward(history, length, grad, wi_f, wo_f)
        return ((carry[0] + dwi, carry[1] + dwo), dx)
    init = (jnp.zeros(wi_f.shape, jnp.float32), jnp.zeros(wo_f.shape, jnp.float32))
    sums, hist_grad = lax.scan(each_user, init, (histories, hist_len, user_grad))
    return (hist_grad, sums[0], sums[1])
```

```python
import jax
import jax.numpy as jnp
from jax import lax
from jax.experimental import pallas as pl
from jax.experimental.pallas import tpu as pltpu
from jax.sharding import PartitionSpec as P

MESH = pl.DeviceIdType.MESH
F32, BF16, I32 = jnp.float32, jnp.bfloat16, jnp.int32
D, HD, L = 1024, 128, 256
RING = (4, 3, 5, 2, 6, 1, 7)
NT = (((1,), (1,)), ((), ()))
TN = (((0,), (0,)), ((), ()))


def mm(a, b, dims=(((1,), (0,)), ((), ()))):
    return lax.dot_general(a, b, dims, preferred_element_type=F32)


def kernel(
    len_s, cnt_v, slot_v, sg_h, hist_h, wi_h, wo_h,
    dx_h, gin_v, gout_v,
    sg, hist, wi, wo, dxb,
    tb, tr, ub, ua, gs1, gr1, gs2, gr2, row1, row2,
    pz, py, xz, xy,
    gate, att, wgt, dsw, pj, dsl, rs, dz, dzr, mvec,
    cb, cr, own, xb, xr, sm, smr, xs, xsr, zb, zr, yb, yr, zs2, zr2, ys2, yr2,
    load, send, recv,
):
    o_id = lax.axis_index("own")
    x = lax.axis_index("rep")
    y, z, c = o_id // 16, (o_id // 2) % 8, o_id % 2

    def at(dy=0, dz_=0, dc=0, dx=0):
        return (((lax.rem(y + dy, 8) * 8 + lax.rem(z + dz_, 8)) * 2 + lax.rem(c + dc, 2)), lax.rem(x + dx, 4))

    def put(src, dst, s, r, dev):
        return pltpu.make_async_remote_copy(
            src_ref=src, dst_ref=dst, send_sem=send.at[s], recv_sem=recv.at[r], device_id=dev, device_id_type=MESH
        )

    loads = [
        pltpu.make_async_copy(a, b, load.at[i])
        for i, (a, b) in enumerate(((sg_h, sg), (hist_h, hist), (wi_h, wi), (wo_h, wo)))
    ]
    for ld in loads:
        ld.start()

    barrier = pltpu.get_barrier_semaphore()
    peers = [at(dc=1)] + [at(dy=k) for k in RING] + [at(dz_=k) for k in RING] + [at(dx=k) for k in (2, 1, 3)]
    for dev in peers:
        pl.semaphore_signal(barrier, 1, device_id=dev, device_id_type=MESH)

    cnt = cnt_v[...].astype(F32)
    slots = slot_v[...].astype(F32).astype(BF16)
    ri = lax.broadcasted_iota(I32, (256, 1), 0)
    lane = lax.broadcasted_iota(I32, (256, 128), 1)
    samp = lax.broadcasted_iota(I32, (256, 256), 1).astype(F32)
    user = lax.rem(ri, 2).astype(F32)
    hi, mid, lo = ri // 128, lax.rem(ri // 16, 8), lax.rem(ri // 2, 8)

    def onehot(ry_, rz_):
        oi = (lax.rem(y + ry_, 8) * 8 + lax.rem(z + rz_, 8)) * 2 + lax.rem(c + 1 - hi + 2, 2)
        off = jnp.sum(jnp.where(lane < oi, cnt, 0.0), axis=1, keepdims=True)
        n = jnp.sum(jnp.where(lane == oi, cnt, 0.0), axis=1, keepdims=True)
        su = mm((lane == oi).astype(F32).astype(BF16), slots, NT)
        d = samp - off
        hit = jnp.zeros((256, 256), F32)
        for k in range(4):
            live = jnp.where((n > k) & (su[:, k : k + 1] == user), 1.0, 0.0)
            hit = hit + jnp.where(d == k, live, 0.0)
        return hit.astype(BF16)

    a1 = onehot(lo, mid)
    a2 = onehot(mid, lo)
    loads[0].wait()
    t1 = mm(a1, sg[:, 0:512])
    tb[0:128, :] = t1[0:128].astype(BF16)
    tb[256:384, :] = t1[128:256].astype(BF16)
    t2 = mm(a2, sg[:, 512:1024])
    tb[128:256, :] = t2[0:128].astype(BF16)
    tb[384:512, :] = t2[128:256].astype(BF16)

    pl.semaphore_wait(barrier, len(peers))
    core_g = put(tb.at[0:256], tr, 0, 0, at(dc=1))
    core_g.start()

    loads[1].wait()
    pr = lax.broadcasted_iota(I32, (256, 1), 0)
    fl = lax.broadcasted_iota(I32, (256, D), 1)

    def order(i, zfirst):
        r = pr + i * 256
        crel, xrel, m8, l8, j = r // 512, lax.rem(r // 128, 4), lax.rem(r // 16, 8), lax.rem(r // 2, 8), lax.rem(r, 2)
        ry_, rz_ = (l8, m8) if zfirst else (m8, l8)
        f = (lax.rem(y + ry_, 8) * 8 + lax.rem(z + rz_, 8)) * 2 + lax.rem(c + 1 - crel + 2, 2)
        f = f * 8 + lax.rem(x + xrel, 4) * 2 + j
        return (fl == f).astype(F32).astype(BF16)

    def permute(zfirst, pm, out):
        def step(i, carry):
            rows = pl.ds(pl.multiple_of(i * 256, 256), 256)
            pm[rows, :] = order(i, zfirst)
            for h in range(2):
                out[rows, h * L : (h + 1) * L] = mm(pm[rows, :], hist[h], NT).astype(BF16)
            return carry

        lax.fori_loop(0, 4, step, 0)

    permute(True, pz, xz)

    core_g.wait_recv()
    ua[...] = tb[256:512, :].astype(F32) + tr[...].astype(F32)
    ub[...] = ua[...].astype(BF16)
    for k in RING:
        a = slice(16 * k, 16 * k + 16)
        b = slice(128 + 16 * k, 128 + 16 * k + 16)
        put(ub.at[a], row1.at[a], 1, 1, at(dz_=k)).start()
        put(ub.at[b], row2.at[a], 2, 2, at(dy=k)).start()

    loads[2].wait()
    loads[3].wait()
    ti = lax.broadcasted_iota(I32, (L, 1), 0)
    tj = lax.broadcasted_iota(I32, (L, L), 1)

    def forward(h, carry):
        n = len_s[h]
        inv = 1.0 / jnp.full((1, 1), n, I32).astype(F32)
        xf = hist[h].astype(F32)
        r = lax.rsqrt(jnp.sum(xf * xf, axis=1, keepdims=True) * (1.0 / D) + 1e-05)
        rs[h] = jnp.broadcast_to(r, (L, HD))
        zz = mm((xf * r).astype(BF16), wi[...])
        sig = 1.0 / (1.0 + jnp.exp(-zz))
        p = zz * sig
        dsl[h] = sig + p * (1.0 - sig)
        gate[h] = p[:, 0:HD]
        pj[h] = p[:, HD:].astype(BF16)
        s = mm(pj[h, :, HD : 2 * HD], pj[h, :, 2 * HD :], NT) * HD**-0.5
        vis = (tj <= ti) & (tj < n)
        ss = 1.0 / (1.0 + jnp.exp(-s))
        sw = s * ss
        wgt[h] = (jnp.where(vis, sw, 0.0) * inv).astype(BF16)
        dsw[h] = jnp.where(vis, ss + sw * (1.0 - ss), 0.0) * (inv * HD**-0.5)
        at_ = mm(wgt[h], pj[h, :, 0:HD])
        att[h] = at_
        keep = jnp.where(ti < n, 1.0, 0.0) * inv
        mixed = (at_ * gate[h]).astype(BF16).astype(F32)
        mvec[h] = jnp.broadcast_to(jnp.sum(mixed * keep, axis=0, keepdims=True), (8, HD))
        return carry

    lax.fori_loop(0, 2, forward, 0)

    put(ub.at[16:128], row1.at[16:128], 1, 1, at(dz_=1)).wait_recv()
    put(ub.at[16:128], row2.at[16:128], 2, 2, at(dy=1)).wait_recv()
    s1, s2 = ua[0:16, :], ua[128:144, :]
    for k in range(1, 8):
        s1 = s1 + row1[16 * k : 16 * k + 16, :].astype(F32)
        s2 = s2 + row2[16 * k : 16 * k + 16, :].astype(F32)
    for k in range(8):
        gs1[k] = s1[2 * k : 2 * k + 2]
        gs2[k] = s2[2 * k : 2 * k + 2]
    for k in RING:
        put(gs1.at[k], gr1.at[k], 3, 3, at(dy=k)).start()
        put(gs2.at[k], gr2.at[k], 4, 4, at(dz_=k)).start()
    gr1[0] = s1[0:2]
    gr2[0] = s2[0:2]

    permute(False, py, xy)

    put(gs1.at[1:8], gr1.at[1:8], 3, 3, at(dy=1)).wait_recv()
    put(gs2.at[1:8], gr2.at[1:8], 4, 4, at(dz_=1)).wait_recv()
    g = jnp.concatenate([jnp.sum(gr1[...], axis=0), jnp.sum(gr2[...], axis=0)], axis=1)
    g8 = jnp.concatenate([g, jnp.zeros((6, D), F32)], axis=0)
    gb = g8.astype(BF16)
    v = mm(gb, wo[...], NT)

    for h in range(2):
        n = len_s[h]
        inv = 1.0 / jnp.full((1, 1), n, I32).astype(F32)
        keep = jnp.where(ti < n, 1.0, 0.0) * inv
        dm = keep * v[h : h + 1, :]
        datt = (dm * gate[h]).astype(BF16)
        dgate = dm * att[h]
        dval = mm(wgt[h], datt, TN)
        ds = (mm(datt, pj[h, :, 0:HD], NT) * dsw[h]).astype(BF16)
        dq = mm(ds, pj[h, :, 2 * HD :])
        dk = mm(ds, pj[h, :, HD : 2 * HD], TN)
        hr = slice(h * L, (h + 1) * L)
        for i, part in enumerate((dgate, dval, dq, dk)):
            cols = slice(i * HD, (i + 1) * HD)
            full = part * dsl[h, :, cols]
            dz[hr, cols] = full.astype(BF16)
            dzr[hr, cols] = (full * rs[h]).astype(BF16)

    cb[0:512, :] = mm(xz[0:512, :], dzr[:, 0:256]).astype(BF16)
    cz = put(cb.at[0:512], cr.at[0:512], 5, 5, at(dc=1))
    cz.start()
    cb[512:1024, :] = mm(xy[0:512, :], dzr[:, 256:512]).astype(BF16)
    cy = put(cb.at[512:1024], cr.at[512:1024], 6, 6, at(dc=1))
    cy.start()
    gp = mm(gb, pz[...], NT)
    m2 = jnp.concatenate([mvec[0, 0:1, :], mvec[1, 0:1, :]], axis=0)
    sm[0:2, :] = gp[0:2, 0:512]
    sm[2:4, 0:HD] = m2
    sm[2:4, HD:512] = jnp.zeros((2, 512 - HD), F32)
    sm[4:8, :] = jnp.zeros((4, 512), F32)
    cs = put(sm, smr, 7, 7, at(dc=1))
    cs.start()
    own[0:512, :] = mm(xz[512:1024, :], dzr[:, 0:256])
    own[512:1024, :] = mm(xy[512:1024, :], dzr[:, 256:512])
    for k in range(4):
        xs[k, 0:2, :] = gp[0:2, 512 + k * HD : 512 + (k + 1) * HD]
        xs[k, 4:6, :] = m2

    cz.wait_recv()
    cy.wait_recv()
    cs.wait_recv()
    for k in (2, 1, 3):
        a = slice(k * 128, (k + 1) * 128)
        b = slice(512 + k * 128, 512 + (k + 1) * 128)
        xb[k, 0:128, :] = (own[a, :] + cr[a, :].astype(F32)).astype(BF16)
        xb[k, 128:256, :] = (own[b, :] + cr[b, :].astype(F32)).astype(BF16)
        put(xb.at[k], xr.at[k], 8, 8, at(dx=k)).start()
    for k in range(4):
        xs[k, 2:4, :] = smr[0:2, k * HD : (k + 1) * HD]
        xs[k, 6:8, :] = smr[2:4, 0:HD]
    for k in (2, 1, 3):
        put(xs.at[k], xsr.at[k], 9, 9, at(dx=k)).start()
    xsr[0] = xs[0]

    def back(h, carry):
        n = len_s[h]
        inv = 1.0 / jnp.full((1, 1), n, I32).astype(F32)
        keep = jnp.where(ti < n, 1.0, 0.0) * inv
        dn = mm(dz[pl.ds(pl.multiple_of(h * L, L), L), :], wi[...], NT)
        r = rs[h, :, 0:1]
        xn = hist[h].astype(F32) * r
        mean = jnp.sum(dn * xn, axis=1, keepdims=True) * (1.0 / D)
        gh = jnp.where(h == 0, g[0:1, :], g[1:2, :])
        dxb[h] = (r * (dn - xn * mean) + keep * gh).astype(BF16)
        return carry

    lax.fori_loop(0, 2, back, 0)
    out = pltpu.make_async_copy(dxb, dx_h, load.at[4])
    out.start()

    put(xb.at[1:4], xr.at[1:4], 8, 8, at(dx=1)).wait_recv()
    put(xs.at[1:4], xsr.at[1:4], 9, 9, at(dx=1)).wait_recv()
    gx = jnp.concatenate([xsr[k, 0:4, :] for k in range(4)], axis=0)
    mx = jnp.concatenate([xsr[k, 4:8, :] for k in range(4)], axis=0)
    sz = own[0:128, :] + cr[0:128, :].astype(F32)
    sy = own[512:640, :] + cr[512:640, :].astype(F32)
    for k in range(1, 4):
        sz = sz + xr[k, 0:128, :].astype(F32)
        sy = sy + xr[k, 128:256, :].astype(F32)
    so = mm(gx.astype(BF16), mx.astype(BF16), TN)
    zb[:, 0:256] = sz.astype(BF16)
    zb[:, 256:384] = so.astype(BF16)
    yb[...] = sy.astype(BF16)
    for k in RING:
        a = slice(16 * k, 16 * k + 16)
        put(zb.at[a], zr.at[a], 10, 10, at(dz_=k)).start()
        put(yb.at[a], yr.at[a], 11, 11, at(dy=k)).start()
    z0 = jnp.concatenate([sz[0:16], so[0:16]], axis=1)
    y0 = sy[0:16]
    put(zb.at[16:128], zr.at[16:128], 10, 10, at(dz_=1)).wait_recv()
    put(yb.at[16:128], yr.at[16:128], 11, 11, at(dy=1)).wait_recv()
    for k in range(1, 8):
        z0 = z0 + zr[16 * k : 16 * k + 16, :].astype(F32)
        y0 = y0 + yr[16 * k : 16 * k + 16, :].astype(F32)
    for k in range(8):
        zs2[k] = z0[2 * k : 2 * k + 2]
        ys2[k] = y0[2 * k : 2 * k + 2]
    for k in RING:
        put(zs2.at[k], zr2.at[k], 12, 12, at(dy=k)).start()
        put(ys2.at[k], yr2.at[k], 13, 13, at(dz_=k)).start()
    zr2[0] = z0[0:2]
    yr2[0] = y0[0:2]

    core_g.wait_send()
    put(ub.at[16:128], row1.at[16:128], 1, 1, at(dz_=1)).wait_send()
    put(ub.at[16:128], row2.at[16:128], 2, 2, at(dy=1)).wait_send()
    put(gs1.at[1:8], gr1.at[1:8], 3, 3, at(dy=1)).wait_send()
    put(gs2.at[1:8], gr2.at[1:8], 4, 4, at(dz_=1)).wait_send()
    cz.wait_send()
    cy.wait_send()
    cs.wait_send()
    put(xb.at[1:4], xr.at[1:4], 8, 8, at(dx=1)).wait_send()
    put(xs.at[1:4], xsr.at[1:4], 9, 9, at(dx=1)).wait_send()
    put(zb.at[16:128], zr.at[16:128], 10, 10, at(dz_=1)).wait_send()
    put(yb.at[16:128], yr.at[16:128], 11, 11, at(dy=1)).wait_send()
    out.wait()

    put(zs2.at[1:8], zr2.at[1:8], 12, 12, at(dy=1)).wait()
    put(ys2.at[1:8], yr2.at[1:8], 13, 13, at(dz_=1)).wait()
    fz = jnp.sum(zr2[...], axis=0)
    fy = jnp.sum(yr2[...], axis=0)
    gin_v[:, 0:256] = fz[:, 0:256]
    gin_v[:, 256:512] = fy
    gout_v[...] = fz[:, 256:384]


def finish(dx_h, gin_h, gout_h, dx_o, gin_o, gout_o, sem):
    copies = [
        pltpu.make_async_copy(a, b, sem.at[i])
        for i, (a, b) in enumerate(((dx_h, dx_o), (gin_h, gin_o), (gout_h, gout_o)))
    ]
    for copy in copies:
        copy.start()
    for copy in copies:
        copy.wait()


def body(sample_grads, send_count, send_user, histories, hist_len, w_in, w_out):
    vm = pl.BlockSpec(memory_space=pltpu.VMEM)
    hbm = pl.BlockSpec(memory_space=pl.ANY)
    sd = jax.ShapeDtypeStruct
    V = pltpu.VMEM
    dx, gin, gout = pl.pallas_call(
        kernel,
        out_shape=(sd((2, L, D), BF16), sd((2, 512), F32), sd((2, HD), F32)),
        in_specs=[pl.BlockSpec(memory_space=pltpu.SMEM), vm, vm, hbm, hbm, hbm, hbm],
        out_specs=(hbm, vm, vm),
        scratch_shapes=[
            V((256, D), BF16), V((2, L, D), BF16), V((D, 512), BF16), V((HD, D), BF16), V((2, L, D), BF16),
            V((512, 512), BF16), V((256, 512), BF16), V((256, 512), BF16), V((256, 512), F32),
            V((8, 2, 512), F32), V((8, 2, 512), F32), V((8, 2, 512), F32), V((8, 2, 512), F32),
            V((128, 512), BF16), V((128, 512), BF16),
            V((D, D), BF16), V((D, D), BF16), V((D, 512), BF16), V((D, 512), BF16),
            V((2, L, HD), F32), V((2, L, HD), F32), V((2, L, L), BF16), V((2, L, L), F32),
            V((2, L, 3 * HD), BF16), V((2, L, 512), F32), V((2, L, HD), F32),
            V((512, 512), BF16), V((512, 512), BF16), V((2, 8, HD), F32),
            V((1024, 256), BF16), V((1024, 256), BF16), V((1024, 256), F32),
            V((4, 256, 256), BF16), V((4, 256, 256), BF16),
            V((8, 512), F32), V((8, 512), F32), V((4, 8, HD), F32), V((4, 8, HD), F32),
            V((128, 384), BF16), V((128, 384), BF16), V((128, 256), BF16), V((128, 256), BF16),
            V((8, 2, 384), F32), V((8, 2, 384), F32), V((8, 2, 256), F32), V((8, 2, 256), F32),
            pltpu.SemaphoreType.DMA((5,)), pltpu.SemaphoreType.DMA((14,)), pltpu.SemaphoreType.DMA((14,)),
        ],
        compiler_params=pltpu.CompilerParams(
            collective_id=0, has_side_effects=True, vmem_limit_bytes=62 * 1024 * 1024
        ),
        name="encoder_backward",
    )(hist_len, send_count, send_user.T, sample_grads, histories, w_in, w_out)
    dx, gin, gout = pl.pallas_call(
        finish,
        out_shape=(sd((2, L, D), BF16), sd((2, 512), F32), sd((2, HD), F32)),
        in_specs=[hbm, hbm, hbm],
        out_specs=(hbm, hbm, hbm),
        scratch_shapes=[pltpu.SemaphoreType.DMA((3,))],
        compiler_params=pltpu.CompilerParams(vmem_limit_bytes=62 * 1024 * 1024),
        name="finish",
    )(dx, gin, gout)
    return dx, gin, gout.T


def solution(mesh):
    both = ("own", "rep")
    return jax.shard_map(
        body,
        mesh=mesh,
        in_specs=(P(both, None), P(both, None), P(both, None), P(both, None, None), P(both), P(), P()),
        out_specs=(P(both, None, None), P(both, None), P(None, both)),
        check_vma=False,
    )
```

```python
import jax
import jax.numpy as jnp
from jax import lax
from jax.experimental import pallas as pl
from jax.experimental.pallas import tpu as pltpu
from jax.sharding import PartitionSpec as P

MESH = pl.DeviceIdType.MESH
F32, BF16, I32 = jnp.float32, jnp.bfloat16, jnp.int32
D, HD, L = 1024, 128, 256
VMEM = 61 * 1024 * 1024
VMEM = 61 * 1024 * 1024
VMEM = 61 * 1024 * 1024
VMEM = 61 * 1024 * 1024
RING = (4, 3, 5, 2, 6, 1, 7)
NT = (((1,), (1,)), ((), ()))
TN = (((0,), (0,)), ((), ()))


def mm(a, b, dims=(((1,), (0,)), ((), ()))):
    return lax.dot_general(a, b, dims, preferred_element_type=F32)


def kernel(
    len_s, cnt_h, slot_h, sg_h, hist_h, wi_h, wo_h,
    dx_o, gin_o, gout_o,
    cnt_v, slot_v, sg, hist, wi, wo,
    tv, vr, vb, vzr, vys, vyr,
    tb, tr, ua, ub, gzr, gys, gyr,
    pz, xz,
    kgate, pre, preg, wgt, dsw, pj, dsl, rs, dz, dzr, mvec, cpre,
    cb, cr, own, xb, xr, sm, smr, xs, xsr, zb, zr, yb, yr, zs2, zr2, ys2, yr2,
    load, send, recv,
):
    o_id = lax.axis_index("own")
    x = lax.axis_index("rep")
    y, z, c = o_id // 16, (o_id // 2) % 8, o_id % 2

    def at(dy=0, dz_=0, dc=0, dx=0):
        return (((lax.rem(y + dy, 8) * 8 + lax.rem(z + dz_, 8)) * 2 + lax.rem(c + dc, 2)), lax.rem(x + dx, 4))

    def put(src, dst, i, dev):
        return pltpu.make_async_remote_copy(
            src_ref=src, dst_ref=dst, send_sem=send.at[i], recv_sem=recv.at[i], device_id=dev, device_id_type=MESH
        )

    def many(src, dst, i, axis, rows=None):
        for k in (2, 1, 3) if axis == "dx" else RING:
            a = k if rows is None else slice(rows * k, rows * k + rows)
            put(src.at[a], dst.at[a], i, at(**{axis: k})).start()

    def whole(src, dst, i, axis, rows=None):
        n = 4 if axis == "dx" else 8
        a = slice(1, n) if rows is None else slice(rows, rows * n)
        return put(src.at[a], dst.at[a], i, at(**{axis: 1}))

    loads = [
        pltpu.make_async_copy(a, b, load.at[i])
        for i, (a, b) in enumerate(
            ((cnt_h, cnt_v), (slot_h, slot_v), (sg_h, sg), (wo_h, wo), (hist_h, hist), (wi_h, wi))
        )
    ]
    for ld in loads:
        ld.start()

    barrier = pltpu.get_barrier_semaphore()
    peers = [at(dc=1)] + [at(dy=k) for k in RING] + [at(dz_=k) for k in RING] + [at(dx=k) for k in (2, 1, 3)]
    for dev in peers:
        pl.semaphore_signal(barrier, 1, device_id=dev, device_id_type=MESH)

    ri = lax.broadcasted_iota(I32, (256, 1), 0)
    lane = lax.broadcasted_iota(I32, (256, 128), 1)
    samp = lax.broadcasted_iota(I32, (256, 256), 1).astype(F32)
    user = lax.rem(ri, 2).astype(F32)
    oi = (lax.rem(y + lax.rem(ri // 2, 8), 8) * 8 + lax.rem(z + lax.rem(ri // 16, 8), 8)) * 2
    oi = oi + lax.rem(c + 1 - ri // 128 + 2, 2)
    loads[0].wait()
    loads[1].wait()
    cnt = cnt_v[...].astype(F32)
    slots = slot_v[...].astype(F32).astype(BF16)
    off = jnp.sum(jnp.where(lane < oi, cnt, 0.0), axis=1, keepdims=True)
    num = jnp.sum(jnp.where(lane == oi, cnt, 0.0), axis=1, keepdims=True)
    su = mm((lane == oi).astype(F32).astype(BF16), slots, NT)
    d = samp - off
    hit = jnp.zeros((256, 256), F32)
    for k in range(4):
        live = jnp.where((num > k) & (su[:, k : k + 1] == user), 1.0, 0.0)
        hit = hit + jnp.where(d == k, live, 0.0)
    hit = hit.astype(BF16)
    loads[2].wait()
    loads[3].wait()
    tv[...] = mm(hit, mm(sg[...], wo[...], NT).astype(BF16))

    pl.semaphore_wait(barrier, len(peers))
    v_core = put(tv.at[0:128], vr, 0, at(dc=1))
    v_core.start()
    tb[...] = mm(hit[0:128], sg[...]).astype(BF16)
    g_core = put(tb, tr, 1, at(dc=1))
    g_core.start()
    ua[...] = mm(hit[128:256], sg[...])
    v_core.wait_recv()
    vb[...] = tv[128:256, :] + vr[...]
    many(vb, vzr, 2, "dz_", 16)
    g_core.wait_recv()
    ua[...] = ua[...] + tr[...].astype(F32)
    ub[...] = ua[...].astype(BF16)
    many(ub, gzr, 3, "dz_", 16)

    loads[4].wait()
    loads[5].wait()
    ti = lax.broadcasted_iota(I32, (L, 1), 0)
    tj = lax.broadcasted_iota(I32, (L, L), 1)

    def shares(h):
        n = len_s[h]
        inv = 1.0 / jnp.full((1, 1), n, I32).astype(F32)
        return n, inv, jnp.where(ti < n, 1.0, 0.0) * inv

    def forward(h, carry):
        n, inv, keep = shares(h)
        xf = hist[h].astype(F32)
        r = lax.rsqrt(jnp.sum(xf * xf, axis=1, keepdims=True) * (1.0 / D) + 1e-05)
        rs[h] = jnp.broadcast_to(r, (L, HD))
        zz = mm((xf * r).astype(BF16), wi[...])
        sig = 1.0 / (1.0 + jnp.exp(-zz))
        p = zz * sig
        ds = sig + p * (1.0 - sig)
        dsl[h] = ds[:, 2 * HD :]
        pj[h] = p[:, HD:].astype(BF16)
        s = mm(pj[h, :, HD : 2 * HD], pj[h, :, 2 * HD :], NT) * HD**-0.5
        vis = (tj <= ti) & (tj < n)
        ss = 1.0 / (1.0 + jnp.exp(-s))
        sw = s * ss
        wgt[h] = (jnp.where(vis, sw, 0.0) * inv).astype(BF16)
        dsw[h] = jnp.where(vis, ss + sw * (1.0 - ss), 0.0) * (inv * HD**-0.5)
        att = mm(wgt[h], pj[h, :, 0:HD])
        mixed = (att * p[:, 0:HD]).astype(BF16).astype(F32)
        mvec[h] = jnp.broadcast_to(jnp.sum(mixed * keep, axis=0, keepdims=True), (8, HD))
        kg = keep * p[:, 0:HD]
        kgate[h] = kg
        pg = keep * att * ds[:, 0:HD]
        pv = mm(wgt[h], kg.astype(BF16), TN) * ds[:, HD : 2 * HD]
        pre[h, :, 0:HD] = pg
        pre[h, :, HD:] = pv
        preg[h, :, 0:HD] = (pg * r).astype(BF16)
        preg[h, :, HD:] = (pv * r).astype(BF16)
        return carry

    lax.fori_loop(0, 2, forward, 0)

    pr = lax.broadcasted_iota(I32, (256, 1), 0)
    fl = lax.broadcasted_iota(I32, (256, D), 1)

    def permute(i, carry):
        r = pr + i * 256
        crel, xrel, j, m8, l8 = r // 512, lax.rem(r // 128, 4), lax.rem(r // 64, 2), lax.rem(r // 8, 8), lax.rem(r, 8)
        ry_, rz_ = jnp.where(j == 0, l8, m8), jnp.where(j == 0, m8, l8)
        f = (lax.rem(y + ry_, 8) * 8 + lax.rem(z + rz_, 8)) * 2 + lax.rem(c + 1 - crel + 2, 2)
        f = f * 8 + lax.rem(x + xrel, 4) * 2 + j
        rows = pl.ds(pl.multiple_of(i * 256, 256), 256)
        pm = (fl == f).astype(F32).astype(BF16)
        pz[rows, :] = pm
        for h in range(2):
            xz[rows, h * L : (h + 1) * L] = mm(pm, hist[h], NT).astype(BF16)
            cpre[h, rows, :] = mm(xz[rows, h * L : (h + 1) * L], preg[h])
        return carry

    lax.fori_loop(0, 2, permute, 0)
    whole(vb, vzr, 2, "dz_", 16).wait_recv()
    s1 = vb[0:16, :]
    for k in range(1, 8):
        s1 = s1 + vzr[16 * k : 16 * k + 16, :]
    for k in range(8):
        vys[k] = s1[2 * k : 2 * k + 2]
    many(vys, vyr, 4, "dy")
    vyr[0] = s1[0:2]

    lax.fori_loop(2, 4, permute, 0)
    whole(ub, gzr, 3, "dz_", 16).wait_recv()
    s1 = ua[0:16, :]
    for k in range(1, 8):
        s1 = s1 + gzr[16 * k : 16 * k + 16, :].astype(F32)
    for k in range(8):
        gys[k] = s1[2 * k : 2 * k + 2]
    many(gys, gyr, 5, "dy")
    gyr[0] = s1[0:2]

    whole(vys, vyr, 4, "dy").wait_recv()
    v = jnp.sum(vyr[...], axis=0)
    va = jnp.concatenate([v[0:1], v[0:1]], axis=1)
    vc = jnp.concatenate([v[1:2], v[1:2]], axis=1)
    cb[0:512, :] = (cpre[0, 0:512, :] * va + cpre[1, 0:512, :] * vc).astype(BF16)
    c1 = put(cb.at[0:512], cr.at[0:512], 6, at(dc=1))
    c1.start()
    for h in range(2):
        datt = (kgate[h] * v[h : h + 1, :]).astype(BF16)
        ds = (mm(datt, pj[h, :, 0:HD], NT) * dsw[h]).astype(BF16)
        dq = mm(ds, pj[h, :, 2 * HD :])
        dk = mm(ds, pj[h, :, HD : 2 * HD], TN)
        hr = slice(h * L, (h + 1) * L)
        for i, part in enumerate((dq, dk)):
            full = part * dsl[h, :, i * HD : (i + 1) * HD]
            dz[hr, (i + 2) * HD : (i + 3) * HD] = full.astype(BF16)
            dzr[hr, i * HD : (i + 1) * HD] = (full * rs[h]).astype(BF16)
    cb[512:1024, :] = mm(xz[0:512, :], dzr[...]).astype(BF16)
    c2 = put(cb.at[512:1024], cr.at[512:1024], 7, at(dc=1))
    c2.start()
    own[0:512, :] = cpre[0, 512:1024, :] * va + cpre[1, 512:1024, :] * vc
    c1.wait_recv()

    def xsums(p, i):
        for k in (2, 1, 3):
            a = slice(p * 512 + k * 128, p * 512 + (k + 1) * 128)
            xb[p, k] = (own[a, :] + cr[a, :].astype(F32)).astype(BF16)
            put(xb.at[p, k], xr.at[p, k], i, at(dx=k)).start()

    xsums(0, 8)
    own[512:1024, :] = mm(xz[512:1024, :], dzr[...])
    c2.wait_recv()
    xsums(1, 9)

    whole(gys, gyr, 5, "dy").wait_recv()
    g = jnp.sum(gyr[...], axis=0)
    gp = mm(jnp.concatenate([g, jnp.zeros((6, D), F32)], axis=0).astype(BF16), pz[...], NT)
    m2 = jnp.concatenate([mvec[0, 0:1, :], mvec[1, 0:1, :]], axis=0)
    sm[0:2, :] = gp[0:2, 0:512]
    sm[2:4, 0:HD] = m2
    sm[2:4, HD:512] = jnp.zeros((2, 512 - HD), F32)
    sm[4:8, :] = jnp.zeros((4, 512), F32)
    cs = put(sm, smr, 10, at(dc=1))
    cs.start()
    for k in range(4):
        xs[k, 0:2, :] = gp[0:2, 512 + k * HD : 512 + (k + 1) * HD]
        xs[k, 4:6, :] = m2

    def back(h, carry):
        n, inv, keep = shares(h)
        hr = pl.ds(pl.multiple_of(h * L, L), L)
        vh = jnp.where(h == 0, va, vc)
        dz[hr, 0 : 2 * HD] = (pre[h] * vh).astype(BF16)
        dn = mm(dz[hr, :], wi[...], NT)
        r = rs[h, :, 0:1]
        xn = hist[h].astype(F32) * r
        mean = jnp.sum(dn * xn, axis=1, keepdims=True) * (1.0 / D)
        gh = jnp.where(h == 0, g[0:1, :], g[1:2, :])
        dx_o[h] = (r * (dn - xn * mean) + keep * gh).astype(BF16)
        return carry

    lax.fori_loop(0, 1, back, 0)
    cs.wait_recv()
    for k in range(4):
        xs[k, 2:4, :] = smr[0:2, k * HD : (k + 1) * HD]
        xs[k, 6:8, :] = smr[2:4, 0:HD]
    many(xs, xsr, 11, "dx")
    xsr[0] = xs[0]
    lax.fori_loop(1, 2, back, 0)

    def xtotal(p, i):
        put(xb.at[p, 1:4], xr.at[p, 1:4], i, at(dx=1)).wait_recv()
        t = own[p * 512 : p * 512 + 128, :] + cr[p * 512 : p * 512 + 128, :].astype(F32)
        for k in range(1, 4):
            t = t + xr[p, k].astype(F32)
        return t

    t0 = xtotal(0, 8)
    whole(xs, xsr, 11, "dx").wait_recv()
    gx = jnp.concatenate([xsr[k, 0:4, :] for k in range(4)], axis=0)
    mx = jnp.concatenate([xsr[k, 4:8, :] for k in range(4)], axis=0)
    so = mm(gx.astype(BF16), mx.astype(BF16), TN)
    t1 = xtotal(1, 9)

    def packed(a):
        p = jnp.concatenate([t0[a], so[a]], axis=1).reshape(8, 8, 384)
        q = jnp.concatenate([t1[a], jnp.zeros((64, HD), F32)], axis=1).reshape(8, 8, 384)
        return jnp.concatenate([p, q], axis=1).reshape(128, 384)

    z0 = packed(slice(0, 64))
    zb[...] = z0.astype(BF16)
    many(zb, zr, 12, "dz_", 16)
    y0 = packed(slice(64, 128))
    yb[...] = y0.astype(BF16)
    many(yb, yr, 13, "dy", 16)

    def total(first, src, dst, i, axis, out, got, j, other):
        whole(src, dst, i, axis, 16).wait_recv()
        t = first[0:16]
        for k in range(1, 8):
            t = t + dst[16 * k : 16 * k + 16, :].astype(F32)
        t = jnp.concatenate([t[0:8, 0:256], t[8:16, 0:256], t[0:8, 256:384]], axis=1)
        for k in range(8):
            out[k] = jnp.broadcast_to(t[k : k + 1], (2, 640))
        many(out, got, j, other)
        got[0] = jnp.broadcast_to(t[0:1], (2, 640))

    total(z0, zb, zr, 12, "dz_", zs2, zr2, 14, "dy")
    total(y0, yb, yr, 13, "dy", ys2, yr2, 15, "dz_")

    for cp in (v_core, g_core, c1, c2, cs):
        cp.wait_send()
    whole(vb, vzr, 2, "dz_", 16).wait_send()
    whole(ub, gzr, 3, "dz_", 16).wait_send()
    whole(vys, vyr, 4, "dy").wait_send()
    whole(gys, gyr, 5, "dy").wait_send()
    put(xb.at[0, 1:4], xr.at[0, 1:4], 8, at(dx=1)).wait_send()
    put(xb.at[1, 1:4], xr.at[1, 1:4], 9, at(dx=1)).wait_send()
    whole(xs, xsr, 11, "dx").wait_send()
    whole(zb, zr, 12, "dz_", 16).wait_send()
    whole(yb, yr, 13, "dy", 16).wait_send()

    whole(zs2, zr2, 14, "dy").wait()
    fz = jnp.sum(zr2[...], axis=0)
    whole(ys2, yr2, 15, "dz_").wait()
    fy = jnp.sum(yr2[...], axis=0)
    gin_o[0:1, :] = fz[0:1, 0:512]
    gin_o[1:2, :] = fy[0:1, 0:512]
    gout_o[0:1, :] = fz[0:1, 512:640]
    gout_o[1:2, :] = fy[0:1, 512:640]


def finish(dx_v, gin_v, gout_v, dx_o, gin_o, gout_o, sem):
    copies = [
        pltpu.make_async_copy(a, b, sem.at[i])
        for i, (a, b) in enumerate(((dx_v, dx_o), (gin_v, gin_o), (gout_v, gout_o)))
    ]
    for copy in copies:
        copy.start()
    for copy in copies:
        copy.wait()


def body(sample_grads, send_count, send_user, histories, hist_len, w_in, w_out):
    vm = pl.BlockSpec(memory_space=pltpu.VMEM)
    hbm = pl.BlockSpec(memory_space=pl.ANY)
    V = pltpu.VMEM
    sd = jax.ShapeDtypeStruct
    dx, gin, gout = pl.pallas_call(
        kernel,
        out_shape=(V((2, L, D), BF16), V((2, 512), F32), V((2, HD), F32)),
        in_specs=[pl.BlockSpec(memory_space=pltpu.SMEM), hbm, hbm, hbm, hbm, hbm, hbm],
        out_specs=(vm, vm, vm),
        scratch_shapes=[
            V((1, 128), I32), V((4, 128), I32), V((256, D), BF16), V((2, L, D), BF16), V((D, 512), BF16), V((HD, D), BF16),
            V((256, HD), F32), V((128, HD), F32), V((128, HD), F32), V((128, HD), F32), V((8, 2, HD), F32), V((8, 2, HD), F32),
            V((128, D), BF16), V((128, D), BF16), V((128, D), F32), V((128, D), BF16), V((128, D), BF16),
            V((8, 2, D), F32), V((8, 2, D), F32),
            V((D, D), BF16), V((D, 512), BF16),
            V((2, L, HD), F32), V((2, L, 256), F32), V((2, L, 256), BF16), V((2, L, L), BF16), V((2, L, L), F32),
            V((2, L, 3 * HD), BF16), V((2, L, 256), F32), V((2, L, HD), F32),
            V((512, 512), BF16), V((512, 256), BF16), V((2, 8, HD), F32), V((2, D, 256), F32),
            V((1024, 256), BF16), V((1024, 256), BF16), V((1024, 256), F32),
            V((2, 4, 128, 256), BF16), V((2, 4, 128, 256), BF16),
            V((8, 512), F32), V((8, 512), F32), V((4, 8, HD), F32), V((4, 8, HD), F32),
            V((128, 384), BF16), V((128, 384), BF16), V((128, 384), BF16), V((128, 384), BF16),
            V((8, 2, 640), F32), V((8, 2, 640), F32), V((8, 2, 640), F32), V((8, 2, 640), F32),
            pltpu.SemaphoreType.DMA((6,)), pltpu.SemaphoreType.DMA((16,)), pltpu.SemaphoreType.DMA((16,)),
        ],
        compiler_params=pltpu.CompilerParams(
            collective_id=0, has_side_effects=True, vmem_limit_bytes=VMEM
        ),
        name="encoder_backward",
    )(hist_len, send_count, send_user.T, sample_grads, histories, w_in, w_out)
    dx, gin, gout = pl.pallas_call(
        finish,
        out_shape=(sd((2, L, D), BF16), sd((2, 512), F32), sd((2, HD), F32)),
        in_specs=[vm, vm, vm],
        out_specs=(hbm, hbm, hbm),
        scratch_shapes=[pltpu.SemaphoreType.DMA((3,))],
        compiler_params=pltpu.CompilerParams(vmem_limit_bytes=8 * 1024 * 1024),
        name="finish",
    )(dx, gin, gout)
    return dx, gin, gout.T


def solution(mesh):
    both = ("own", "rep")
    return jax.shard_map(
        body,
        mesh=mesh,
        in_specs=(P(both, None), P(both, None), P(both, None), P(both, None, None), P(both), P(), P()),
        out_specs=(P(both, None, None), P(both, None), P(None, both)),
        check_vma=False,
    )
```

```python
import jax
import jax.numpy as jnp
from jax import lax
from jax.experimental import pallas as pl
from jax.experimental.pallas import tpu as pltpu
from jax.sharding import PartitionSpec as P

MESH = pl.DeviceIdType.MESH
F32, BF16, I32 = jnp.float32, jnp.bfloat16, jnp.int32
D, HD, L = 1024, 128, 256
VMEM = 61 * 1024 * 1024
RING = (4, 3, 5, 2, 6, 1, 7)
NT = (((1,), (1,)), ((), ()))
TN = (((0,), (0,)), ((), ()))


def mm(a, b, dims=(((1,), (0,)), ((), ()))):
    return lax.dot_general(a, b, dims, preferred_element_type=F32)


def kernel(
    len_s, cnt_h, slot_h, sg_h, hist_h, wi_h, wo_h,
    dx_o, gin_o, gout_o,
    cnt_v, slot_v, sg, hist, wi, wo,
    tv, tvb, vzr, vys, vyr, vfin,
    tb, tr, ua, ub, gzr, gys, gyr,
    pz, xz,
    kgate, pre, preg, wgt, dsw, pj, dsl, rs, dz, dzr, mvec, cpre,
    cb, cr, own, xb, xr, gm, gmr, fbt, fb, fr,
    load, send, recv,
):
    o_id = lax.axis_index("own")
    x = lax.axis_index("rep")
    y, z, c = o_id // 16, (o_id // 2) % 8, o_id % 2

    def at(dy=0, dz_=0, dc=0, dx=0, core=None):
        k = lax.rem(c + dc, 2) if core is None else core
        return (lax.rem(y + dy, 8) * 8 + lax.rem(z + dz_, 8)) * 2 + k, lax.rem(x + dx, 4)

    def put(src, dst, i, dev):
        return pltpu.make_async_remote_copy(
            src_ref=src, dst_ref=dst, send_sem=send.at[i], recv_sem=recv.at[i], device_id=dev, device_id_type=MESH
        )

    def many(src, dst, i, axis, rows=None):
        for k in (2, 1, 3) if axis == "dx" else RING:
            a = k if rows is None else slice(rows * k, rows * k + rows)
            put(src.at[a], dst.at[a], i, at(**{axis: k})).start()

    def whole(src, dst, i, axis, rows=None):
        n = 4 if axis == "dx" else 8
        a = slice(1, n) if rows is None else slice(rows, rows * n)
        return put(src.at[a], dst.at[a], i, at(**{axis: 1}))

    loads = [
        pltpu.make_async_copy(a, b, load.at[i])
        for i, (a, b) in enumerate(
            ((cnt_h, cnt_v), (slot_h, slot_v), (sg_h, sg), (wo_h, wo), (hist_h, hist), (wi_h, wi))
        )
    ]
    for ld in loads:
        ld.start()

    barrier = pltpu.get_barrier_semaphore()
    peers = [at(dc=1)] + [at(dy=k) for k in RING] + [at(dz_=k) for k in RING] + [at(dx=k) for k in (2, 1, 3)]
    for dev in peers:
        pl.semaphore_signal(barrier, 1, device_id=dev, device_id_type=MESH)

    @pl.when(c == 1)
    def _():
        for k in RING:
            pl.semaphore_signal(barrier, 1, device_id=at(dz_=k, core=0), device_id_type=MESH)

    ri = lax.broadcasted_iota(I32, (256, 1), 0)
    lane = lax.broadcasted_iota(I32, (256, 128), 1)
    samp = lax.broadcasted_iota(I32, (256, 256), 1).astype(F32)
    user = lax.rem(ri, 2).astype(F32)
    loads[0].wait()
    loads[1].wait()
    cnt = cnt_v[...].astype(F32)
    slots = slot_v[...].astype(F32).astype(BF16)

    def onehot(ry_, rz_, core):
        oi = (lax.rem(y + ry_, 8) * 8 + lax.rem(z + rz_, 8)) * 2 + core
        off = jnp.sum(jnp.where(lane < oi, cnt, 0.0), axis=1, keepdims=True)
        num = jnp.sum(jnp.where(lane == oi, cnt, 0.0), axis=1, keepdims=True)
        su = mm((lane == oi).astype(F32).astype(BF16), slots, NT)
        d = samp - off
        hit = jnp.zeros((256, 256), F32)
        for k in range(4):
            live = jnp.where((num > k) & (su[:, k : k + 1] == user), 1.0, 0.0)
            hit = hit + jnp.where(d == k, live, 0.0)
        return hit.astype(BF16)

    hit = onehot(lax.rem(ri // 4, 8), ri // 32, lax.rem(ri // 2, 2))
    loads[2].wait()
    loads[3].wait()
    tv[...] = mm(hit, mm(sg[...], wo[...], NT).astype(BF16))
    tvb[...] = tv[...].astype(BF16)

    def vput(k):
        slot = pl.ds(pl.multiple_of((k + 7 * c) * 32, 32), 32)
        return put(tvb.at[32 * k : 32 * k + 32], vzr.at[slot], 0, at(dz_=k, core=1))

    pl.semaphore_wait(barrier, len(peers) + 7 * (1 - c))
    for k in RING:
        vput(k).start()

    @pl.when(c == 0)
    def _():
        put(tvb.at[0:32], vzr.at[0:32], 0, at(dc=1)).start()

    hit = onehot(lax.rem(ri // 2, 8), lax.rem(ri // 16, 8), lax.rem(c + 1 - ri // 128 + 2, 2))
    tb[...] = mm(hit[0:128], sg[...]).astype(BF16)
    g_core = put(tb, tr, 1, at(dc=1))
    g_core.start()
    ua[...] = mm(hit[128:256], sg[...])
    g_core.wait_recv()
    ua[...] = ua[...] + tr[...].astype(F32)
    ub[...] = ua[...].astype(BF16)
    many(ub, gzr, 3, "dz_", 16)

    loads[4].wait()
    loads[5].wait()
    ti = lax.broadcasted_iota(I32, (L, 1), 0)
    tj = lax.broadcasted_iota(I32, (L, L), 1)

    def shares(h):
        n = len_s[h]
        inv = 1.0 / jnp.full((1, 1), n, I32).astype(F32)
        return n, inv, jnp.where(ti < n, 1.0, 0.0) * inv

    def forward(h, carry):
        n, inv, keep = shares(h)
        xf = hist[h].astype(F32)
        r = lax.rsqrt(jnp.sum(xf * xf, axis=1, keepdims=True) * (1.0 / D) + 1e-05)
        rs[h] = jnp.broadcast_to(r, (L, HD))
        zz = mm((xf * r).astype(BF16), wi[...])
        sig = 1.0 / (1.0 + jnp.exp(-zz))
        p = zz * sig
        ds = sig + p * (1.0 - sig)
        dsl[h] = ds[:, 2 * HD :]
        pj[h] = p[:, HD:].astype(BF16)
        s = mm(pj[h, :, HD : 2 * HD], pj[h, :, 2 * HD :], NT) * HD**-0.5
        vis = (tj <= ti) & (tj < n)
        ss = 1.0 / (1.0 + jnp.exp(-s))
        sw = s * ss
        wgt[h] = (jnp.where(vis, sw, 0.0) * inv).astype(BF16)
        dsw[h] = jnp.where(vis, ss + sw * (1.0 - ss), 0.0) * (inv * HD**-0.5)
        att = mm(wgt[h], pj[h, :, 0:HD])
        mixed = (att * p[:, 0:HD]).astype(BF16).astype(F32)
        mvec[h] = jnp.broadcast_to(jnp.sum(mixed * keep, axis=0, keepdims=True), (8, HD))
        kg = keep * p[:, 0:HD]
        kgate[h] = kg
        pg = keep * att * ds[:, 0:HD]
        pv = mm(wgt[h], kg.astype(BF16), TN) * ds[:, HD : 2 * HD]
        pre[h, :, 0:HD] = pg
        pre[h, :, HD:] = pv
        preg[h, :, 0:HD] = (pg * r).astype(BF16)
        preg[h, :, HD:] = (pv * r).astype(BF16)
        return carry

    lax.fori_loop(0, 2, forward, 0)

    pr = lax.broadcasted_iota(I32, (256, 1), 0)
    fl = lax.broadcasted_iota(I32, (256, D), 1)

    def permute(i, carry):
        r = pr + i * 256
        crel, xrel, ry_, rz_, j = r // 512, lax.rem(r // 128, 4), lax.rem(r // 16, 8), lax.rem(r // 2, 8), lax.rem(r, 2)
        f = (lax.rem(y + ry_, 8) * 8 + lax.rem(z + rz_, 8)) * 2 + lax.rem(c + 1 - crel + 2, 2)
        f = f * 8 + lax.rem(x + xrel, 4) * 2 + j
        rows = pl.ds(pl.multiple_of(i * 256, 256), 256)
        pm = (fl == f).astype(F32).astype(BF16)
        pz[rows, :] = pm
        for h in range(2):
            xz[rows, h * L : (h + 1) * L] = mm(pm, hist[h], NT).astype(BF16)
            cpre[h, rows, :] = mm(xz[rows, h * L : (h + 1) * L], preg[h])
        return carry

    lax.fori_loop(0, 2, permute, 0)

    @pl.when(c == 1)
    def _():
        put(vzr.at[0:480], vzr.at[0:480], 0, at(dc=1)).wait_recv()
        s = tv[0:32, :]
        for k in range(15):
            s = s + vzr[32 * k : 32 * k + 32, :].astype(F32)
        for k in range(8):
            vys[k] = s[4 * k : 4 * k + 4]
        many(vys, vyr, 2, "dy")
        vyr[0] = s[0:4]

    lax.fori_loop(2, 4, permute, 0)
    v_core = put(vfin, vfin, 4, at(dc=1))

    @pl.when(c == 1)
    def _():
        whole(vys, vyr, 2, "dy").wait_recv()
        vfin[...] = jnp.sum(vyr[...], axis=0)
        v_core.start()

    @pl.when(c == 0)
    def _():
        v_core.wait_recv()

    v = jnp.where(c == 0, vfin[0:2, :], vfin[2:4, :])
    va = jnp.concatenate([v[0:1], v[0:1]], axis=1)
    vc = jnp.concatenate([v[1:2], v[1:2]], axis=1)
    cb[0:512, :] = (cpre[0, 0:512, :] * va + cpre[1, 0:512, :] * vc).astype(BF16)
    c1 = put(cb.at[0:512], cr.at[0:512], 6, at(dc=1))
    c1.start()
    whole(ub, gzr, 3, "dz_", 16).wait_recv()
    s1 = ua[0:16, :]
    for k in range(1, 8):
        s1 = s1 + gzr[16 * k : 16 * k + 16, :].astype(F32)
    for k in range(8):
        gys[k] = s1[2 * k : 2 * k + 2]
    many(gys, gyr, 5, "dy")
    gyr[0] = s1[0:2]
    for h in range(2):
        datt = (kgate[h] * v[h : h + 1, :]).astype(BF16)
        ds = (mm(datt, pj[h, :, 0:HD], NT) * dsw[h]).astype(BF16)
        dq = mm(ds, pj[h, :, 2 * HD :])
        dk = mm(ds, pj[h, :, HD : 2 * HD], TN)
        hr = slice(h * L, (h + 1) * L)
        for i, part in enumerate((dq, dk)):
            full = part * dsl[h, :, i * HD : (i + 1) * HD]
            dz[hr, (i + 2) * HD : (i + 3) * HD] = full.astype(BF16)
            dzr[hr, i * HD : (i + 1) * HD] = (full * rs[h]).astype(BF16)
    cb[512:1024, :] = mm(xz[0:512, :], dzr[...]).astype(BF16)
    c2 = put(cb.at[512:1024], cr.at[512:1024], 7, at(dc=1))
    c2.start()
    own[0:512, :] = cpre[0, 512:1024, :] * va + cpre[1, 512:1024, :] * vc
    c1.wait_recv()

    def xsums(p, i):
        for k in (2, 1, 3):
            a = slice(p * 512 + k * 128, p * 512 + (k + 1) * 128)
            xb[p, k] = (own[a, :] + cr[a, :].astype(F32)).astype(BF16)
            put(xb.at[p, k], xr.at[p, k], i, at(dx=k)).start()

    xsums(0, 8)
    own[512:1024, :] = mm(xz[512:1024, :], dzr[...])
    c2.wait_recv()
    xsums(1, 9)

    whole(gys, gyr, 5, "dy").wait_recv()
    g = jnp.sum(gyr[...], axis=0)
    gp = mm(jnp.concatenate([g, jnp.zeros((6, D), F32)], axis=0).astype(BF16), pz[...], NT)
    m2 = jnp.concatenate([mvec[0, 0:1, :], mvec[1, 0:1, :]], axis=0)
    for dc in range(2):
        for dx in range(4):
            q = (1 - dc) * 4 + dx
            gm[dc * 4 + dx, 0:2, :] = gp[0:2, q * HD : (q + 1) * HD]
            gm[dc * 4 + dx, 2:4, :] = m2
    for k in (6, 2, 5, 7, 1, 3, 4):
        put(gm.at[k], gmr.at[k], 10, at(dc=k // 4, dx=k % 4)).start()
    gmr[0] = gm[0]

    def back(h, carry):
        n, inv, keep = shares(h)
        hr = pl.ds(pl.multiple_of(h * L, L), L)
        vh = jnp.where(h == 0, va, vc)
        dz[hr, 0 : 2 * HD] = (pre[h] * vh).astype(BF16)
        dn = mm(dz[hr, :], wi[...], NT)
        r = rs[h, :, 0:1]
        xn = hist[h].astype(F32) * r
        mean = jnp.sum(dn * xn, axis=1, keepdims=True) * (1.0 / D)
        gh = jnp.where(h == 0, g[0:1, :], g[1:2, :])
        dx_o[h] = (r * (dn - xn * mean) + keep * gh).astype(BF16)
        return carry

    lax.fori_loop(0, 2, back, 0)

    def xtotal(p, i):
        put(xb.at[p, 1:4], xr.at[p, 1:4], i, at(dx=1)).wait_recv()
        t = own[p * 512 : p * 512 + 128, :] + cr[p * 512 : p * 512 + 128, :].astype(F32)
        for k in range(1, 4):
            t = t + xr[p, k].astype(F32)
        return t

    t0 = xtotal(0, 8)
    t1 = xtotal(1, 9)
    put(gm.at[1:8], gmr.at[1:8], 10, at(dc=1)).wait_recv()
    gx = jnp.concatenate([gmr[k, 0:2, :] for k in range(8)], axis=0)
    mx = jnp.concatenate([gmr[k, 2:4, :] for k in range(8)], axis=0)
    so = mm(gx.astype(BF16), mx.astype(BF16), TN)
    t = jnp.concatenate([t0, t1, so], axis=1)
    fbt[...] = t.astype(BF16)
    for a in RING + (0,):
        for b in RING + (0,):
            k = a * 8 + b
            if k:
                fb[k] = fbt[2 * k : 2 * k + 2, :]
                put(fb.at[k], fr.at[k], 11, at(dy=a, dz_=b)).start()

    @pl.when(c == 0)
    def _():
        put(tvb, tvb, 0, at(dc=1)).wait_send()

    @pl.when(c == 1)
    def _():
        put(tvb.at[32:256], tvb.at[32:256], 0, at(dc=1)).wait_send()
        whole(vys, vyr, 2, "dy").wait_send()
        v_core.wait_send()

    for cp in (g_core, c1, c2):
        cp.wait_send()
    whole(ub, gzr, 3, "dz_", 16).wait_send()
    whole(gys, gyr, 5, "dy").wait_send()
    put(xb.at[0, 1:4], xr.at[0, 1:4], 8, at(dx=1)).wait_send()
    put(xb.at[1, 1:4], xr.at[1, 1:4], 9, at(dx=1)).wait_send()
    put(gm.at[1:8], gmr.at[1:8], 10, at(dc=1)).wait_send()

    put(fb.at[1:64], fr.at[1:64], 11, at(dy=1)).wait()
    f = t[0:2, :] + jnp.sum(fr[1:64].astype(F32), axis=0)
    gin_o[...] = f[:, 0:512]
    gout_o[...] = f[:, 512:640]


def finish(dx_v, gin_v, gout_v, dx_o, gin_o, gout_o, sem):
    pairs = [(dx_v.at[h, r : r + 128], dx_o.at[h, r : r + 128]) for h in range(2) for r in (0, 128)]
    pairs += [(gin_v, gin_o), (gout_v, gout_o)]
    copies = [pltpu.make_async_copy(a, b, sem.at[i]) for i, (a, b) in enumerate(pairs)]
    for copy in copies:
        copy.start()
    for copy in copies:
        copy.wait()


def body(sample_grads, send_count, send_user, histories, hist_len, w_in, w_out):
    vm = pl.BlockSpec(memory_space=pltpu.VMEM)
    hbm = pl.BlockSpec(memory_space=pl.ANY)
    V = pltpu.VMEM
    sd = jax.ShapeDtypeStruct
    dx, gin, gout = pl.pallas_call(
        kernel,
        out_shape=(V((2, L, D), BF16), V((2, 512), F32), V((2, HD), F32)),
        in_specs=[pl.BlockSpec(memory_space=pltpu.SMEM), hbm, hbm, hbm, hbm, hbm, hbm],
        out_specs=(vm, vm, vm),
        scratch_shapes=[
            V((1, 128), I32), V((4, 128), I32), V((256, D), BF16), V((2, L, D), BF16), V((D, 512), BF16), V((HD, D), BF16),
            V((256, HD), F32), V((256, HD), BF16), V((480, HD), BF16), V((8, 4, HD), F32), V((8, 4, HD), F32), V((4, HD), F32),
            V((128, D), BF16), V((128, D), BF16), V((128, D), F32), V((128, D), BF16), V((128, D), BF16),
            V((8, 2, D), F32), V((8, 2, D), F32),
            V((D, D), BF16), V((D, 512), BF16),
            V((2, L, HD), F32), V((2, L, 256), F32), V((2, L, 256), BF16), V((2, L, L), BF16), V((2, L, L), F32),
            V((2, L, 3 * HD), BF16), V((2, L, 256), F32), V((2, L, HD), F32),
            V((512, 512), BF16), V((512, 256), BF16), V((2, 8, HD), F32), V((2, D, 256), F32),
            V((1024, 256), BF16), V((1024, 256), BF16), V((1024, 256), F32),
            V((2, 4, 128, 256), BF16), V((2, 4, 128, 256), BF16),
            V((8, 4, HD), F32), V((8, 4, HD), F32), V((128, 640), BF16), V((64, 2, 640), BF16), V((64, 2, 640), BF16),
            pltpu.SemaphoreType.DMA((6,)), pltpu.SemaphoreType.DMA((12,)), pltpu.SemaphoreType.DMA((12,)),
        ],
        compiler_params=pltpu.CompilerParams(
            collective_id=0, has_side_effects=True, vmem_limit_bytes=VMEM
        ),
        name="encoder_backward",
    )(hist_len, send_count, send_user.T, sample_grads, histories, w_in, w_out)
    dx, gin, gout = pl.pallas_call(
        finish,
        out_shape=(sd((2, L, D), BF16), sd((2, 512), F32), sd((2, HD), F32)),
        in_specs=[vm, vm, vm],
        out_specs=(hbm, hbm, hbm),
        scratch_shapes=[pltpu.SemaphoreType.DMA((6,))],
        compiler_params=pltpu.CompilerParams(vmem_limit_bytes=8 * 1024 * 1024),
        name="finish",
    )(dx, gin, gout)
    return dx, gin, gout.T


def solution(mesh):
    both = ("own", "rep")
    return jax.shard_map(
        body,
        mesh=mesh,
        in_specs=(P(both, None), P(both, None), P(both, None), P(both, None, None), P(both), P(), P()),
        out_specs=(P(both, None, None), P(both, None), P(None, both)),
        check_vma=False,
    )
```

```python
import jax
import jax.numpy as jnp
from jax import lax
from jax.experimental import pallas as pl
from jax.experimental.pallas import tpu as pltpu
from jax.sharding import PartitionSpec as P

MESH = pl.DeviceIdType.MESH
F32, BF16, I32 = jnp.float32, jnp.bfloat16, jnp.int32
D, HD, L = 1024, 128, 256
VMEM = 61 * 1024 * 1024
RING = (4, 3, 5, 2, 6, 1, 7)
NT = (((1,), (1,)), ((), ()))
TN = (((0,), (0,)), ((), ()))


def mm(a, b, dims=(((1,), (0,)), ((), ()))):
    return lax.dot_general(a, b, dims, preferred_element_type=F32)


def kernel(
    len_s, cnt_h, slot_h, sg_h, hist_h, wi_h, wo_h,
    dx_o, gin_o, gout_o,
    cnt_v, slot_v, sg, hist, wi, wo,
    tv, tvb, vzr, vys, vyr, vfin,
    tb, tr, ua, ub, gzr, gys, gyr,
    pz, xz, xq,
    kgate, pre, preg, wgt, dsw, pj, dsl, rs, dz, dzr, mvec, cpre,
    cb, cr, own, kc, kcr, kown, xb, xr, kb, kr, gm, gmr, fbt, fb, fr, kf, kfr,
    load, send, recv,
):
    o_id = lax.axis_index("own")
    x = lax.axis_index("rep")
    y, z, c = o_id // 16, (o_id // 2) % 8, o_id % 2

    def at(dy=0, dz_=0, dc=0, dx=0, core=None):
        k = lax.rem(c + dc, 2) if core is None else core
        return (lax.rem(y + dy, 8) * 8 + lax.rem(z + dz_, 8)) * 2 + k, lax.rem(x + dx, 4)

    def put(src, dst, i, dev):
        return pltpu.make_async_remote_copy(
            src_ref=src, dst_ref=dst, send_sem=send.at[i], recv_sem=recv.at[i], device_id=dev, device_id_type=MESH
        )

    def many(src, dst, i, axis, rows=None):
        for k in (2, 1, 3) if axis == "dx" else RING:
            a = k if rows is None else slice(rows * k, rows * k + rows)
            put(src.at[a], dst.at[a], i, at(**{axis: k})).start()

    def whole(src, dst, i, axis, rows=None):
        n = 4 if axis == "dx" else 8
        a = slice(1, n) if rows is None else slice(rows, rows * n)
        return put(src.at[a], dst.at[a], i, at(**{axis: 1}))

    def fetch(i, src, dst):
        cp = pltpu.make_async_copy(src, dst, load.at[i])
        cp.start()
        return cp

    small = [fetch(0, cnt_h, cnt_v), fetch(1, slot_h, slot_v)]
    for k in range(0, 256, 64):
        pltpu.make_async_copy(sg_h.at[k : k + 64], sg.at[k : k + 64], load.at[2]).start()
    small += [pltpu.make_async_copy(sg_h, sg, load.at[2]), fetch(3, wo_h, wo)]

    barrier = pltpu.get_barrier_semaphore()
    peers = [at(dc=1)] + [at(dy=k) for k in RING] + [at(dz_=k) for k in RING] + [at(dx=k) for k in (2, 1, 3)]
    for dev in peers:
        pl.semaphore_signal(barrier, 1, device_id=dev, device_id_type=MESH)

    @pl.when(c == 1)
    def _():
        for k in RING:
            pl.semaphore_signal(barrier, 1, device_id=at(dz_=k, core=0), device_id_type=MESH)

    large = [fetch(4, hist_h, hist), fetch(5, wi_h, wi)]

    ri = lax.broadcasted_iota(I32, (256, 1), 0)
    lane = lax.broadcasted_iota(I32, (256, 128), 1)
    samp = lax.broadcasted_iota(I32, (256, 256), 1).astype(F32)
    user = lax.rem(ri, 2).astype(F32)
    for cp in small:
        cp.wait()
    cnt = cnt_v[...].astype(F32)
    slots = slot_v[...].astype(F32).astype(BF16)

    def onehot(ry_, rz_, core):
        oi = (lax.rem(y + ry_, 8) * 8 + lax.rem(z + rz_, 8)) * 2 + core
        off = jnp.sum(jnp.where(lane < oi, cnt, 0.0), axis=1, keepdims=True)
        num = jnp.sum(jnp.where(lane == oi, cnt, 0.0), axis=1, keepdims=True)
        su = mm((lane == oi).astype(F32).astype(BF16), slots, NT)
        d = samp - off
        hit = jnp.zeros((256, 256), F32)
        for k in range(4):
            live = jnp.where((num > k) & (su[:, k : k + 1] == user), 1.0, 0.0)
            hit = hit + jnp.where(d == k, live, 0.0)
        return hit.astype(BF16)

    hit = onehot(lax.rem(ri // 4, 8), ri // 32, lax.rem(ri // 2, 2))
    tv[...] = mm(hit, mm(sg[...], wo[...], NT).astype(BF16))
    tvb[...] = tv[...].astype(BF16)

    def vput(k):
        slot = pl.ds(pl.multiple_of((k + 7 * c) * 32, 32), 32)
        return put(tvb.at[32 * k : 32 * k + 32], vzr.at[slot], 0, at(dz_=k, core=1))

    pl.semaphore_wait(barrier, len(peers) + 7 * (1 - c))
    for k in RING:
        vput(k).start()

    @pl.when(c == 0)
    def _():
        put(tvb.at[0:32], vzr.at[0:32], 0, at(dc=1)).start()

    hit = onehot(lax.rem(ri // 2, 8), lax.rem(ri // 16, 8), lax.rem(c + 1 - ri // 128 + 2, 2))
    sr = lax.broadcasted_iota(I32, (128, 1), 0)
    sl = lax.broadcasted_iota(I32, (128, 128), 1)
    swap = (sl == lax.rem(sr // 2, 8) * 16 + sr // 16 * 2 + lax.rem(sr, 2)).astype(F32).astype(BF16)
    other = jnp.concatenate([mm(swap, hit[0:128]), mm(swap, hit[128:256])], axis=0).astype(BF16)
    tb[0:128, :] = mm(hit[0:128], sg[:, 0:512]).astype(BF16)
    tb[128:256, :] = mm(other[0:128], sg[:, 512:]).astype(BF16)
    g_core = put(tb, tr, 1, at(dc=1))
    g_core.start()
    ua[0:128, :] = mm(hit[128:256], sg[:, 0:512])
    ua[128:256, :] = mm(other[128:256], sg[:, 512:])

    for cp in large:
        cp.wait()
    ti = lax.broadcasted_iota(I32, (L, 1), 0)
    tj = lax.broadcasted_iota(I32, (L, L), 1)

    def shares(h):
        n = len_s[h]
        inv = 1.0 / jnp.full((1, 1), n, I32).astype(F32)
        return n, inv, jnp.where(ti < n, 1.0, 0.0) * inv

    def forward(h, carry):
        n, inv, keep = shares(h)
        xf = hist[h].astype(F32)
        r = lax.rsqrt(jnp.sum(xf * xf, axis=1, keepdims=True) * (1.0 / D) + 1e-05)
        rs[h] = jnp.broadcast_to(r, (L, HD))
        zz = mm((xf * r).astype(BF16), wi[...])
        sig = 1.0 / (1.0 + jnp.exp(-zz))
        p = zz * sig
        ds = sig + p * (1.0 - sig)
        dsl[h] = ds[:, 2 * HD :]
        pj[h] = p[:, HD:].astype(BF16)
        s = mm(pj[h, :, HD : 2 * HD], pj[h, :, 2 * HD :], NT) * HD**-0.5
        vis = (tj <= ti) & (tj < n)
        ss = 1.0 / (1.0 + jnp.exp(-s))
        sw = s * ss
        wgt[h] = (jnp.where(vis, sw, 0.0) * inv).astype(BF16)
        dsw[h] = jnp.where(vis, ss + sw * (1.0 - ss), 0.0) * (inv * HD**-0.5)
        att = mm(wgt[h], pj[h, :, 0:HD])
        mixed = (att * p[:, 0:HD]).astype(BF16).astype(F32)
        mvec[h] = jnp.broadcast_to(jnp.sum(mixed * keep, axis=0, keepdims=True), (8, HD))
        kg = keep * p[:, 0:HD]
        kgate[h] = kg
        pg = keep * att * ds[:, 0:HD]
        pv = mm(wgt[h], kg.astype(BF16), TN) * ds[:, HD : 2 * HD]
        pre[h, :, 0:HD] = pg
        pre[h, :, HD:] = pv
        preg[h, :, 0:HD] = (pg * r).astype(BF16)
        preg[h, :, HD:] = (pv * r).astype(BF16)
        return carry

    lax.fori_loop(0, 1, forward, 0)
    g_core.wait_recv()
    ua[...] = ua[...] + tr[...].astype(F32)
    ub[...] = ua[...].astype(BF16)
    many(ub, gzr, 3, "dz_", 16)
    many(ub.at[128:256], gzr.at[128:256], 15, "dy", 16)
    lax.fori_loop(1, 2, forward, 0)


    @pl.when(c == 1)
    def _():
        put(vzr.at[0:480], vzr.at[0:480], 0, at(dc=1)).wait_recv()
        s = tv[0:32, :]
        for k in range(15):
            s = s + vzr[32 * k : 32 * k + 32, :].astype(F32)
        for k in range(8):
            vys[k] = s[4 * k : 4 * k + 4]
        many(vys, vyr, 2, "dy")
        vyr[0] = s[0:4]

    pr = lax.broadcasted_iota(I32, (512, 1), 0)
    fl = lax.broadcasted_iota(I32, (512, D), 1)

    def permute(i, carry):
        r = pr + i * 512
        crel, xrel, ry_, rz_, j = r // 512, lax.rem(r // 128, 4), lax.rem(r // 16, 8), lax.rem(r // 2, 8), lax.rem(r, 2)
        f = (lax.rem(y + ry_, 8) * 8 + lax.rem(z + rz_, 8)) * 2 + lax.rem(c + 1 - crel + 2, 2)
        f = f * 8 + lax.rem(x + xrel, 4) * 2 + j
        rows = pl.ds(pl.multiple_of(i * 512, 512), 512)
        pm = (fl == f).astype(F32).astype(BF16)
        pz[rows, :] = pm
        xz[rows, :] = mm(pm, hist[...].reshape(2 * L, D), NT).astype(BF16)
        for h in range(2):
            cpre[h, rows, :] = mm(xz[rows, h * L : (h + 1) * L], preg[h])
        return carry

    lax.fori_loop(0, 2, permute, 0)
    for k in range(0, D, 128):
        xq[k : k + 128, :] = mm(swap, xz[k : k + 128, :]).astype(BF16)

    whole(ub, gzr, 3, "dz_", 16).wait_recv()
    whole(ub.at[128:256], gzr.at[128:256], 15, "dy", 16).wait_recv()
    mine = []
    for p, i, axis in ((0, 5, "dy"), (1, 16, "dz_")):
        s1 = ua[128 * p : 128 * p + 16, :]
        for k in range(1, 8):
            s1 = s1 + gzr[128 * p + 16 * k : 128 * p + 16 * k + 16, :].astype(F32)
        mine.append(s1[0:2])
        s1 = s1.astype(BF16)
        for k in range(1, 8):
            gys[p, k] = s1[2 * k : 2 * k + 2]
        many(gys.at[p], gyr.at[p], i, axis)

    v_core = put(vfin, vfin, 4, at(dc=1))

    @pl.when(c == 1)
    def _():
        whole(vys, vyr, 2, "dy").wait_recv()
        vfin[...] = jnp.sum(vyr[...], axis=0)
        v_core.start()

    @pl.when(c == 0)
    def _():
        v_core.wait_recv()

    v = jnp.where(c == 0, vfin[0:2, :], vfin[2:4, :])
    va = jnp.concatenate([v[0:1], v[0:1]], axis=1)
    vc = jnp.concatenate([v[1:2], v[1:2]], axis=1)
    for h in range(2):
        datt = (kgate[h] * v[h : h + 1, :]).astype(BF16)
        ds = (mm(datt, pj[h, :, 0:HD], NT) * dsw[h]).astype(BF16)
        dq = mm(ds, pj[h, :, 2 * HD :])
        dk = mm(ds, pj[h, :, HD : 2 * HD], TN)
        hr = slice(h * L, (h + 1) * L)
        for i, part in enumerate((dq, dk)):
            full = part * dsl[h, :, i * HD : (i + 1) * HD]
            dz[hr, (i + 2) * HD : (i + 3) * HD] = full.astype(BF16)
            dzr[hr, i * HD : (i + 1) * HD] = (full * rs[h]).astype(BF16)

    def regroup(r):
        return jnp.concatenate([r[a * 128 + b * 16 : a * 128 + b * 16 + 16] for b in range(8) for a in range(4)], axis=0)

    kc[0:512, :] = regroup(mm(xz[0:512, :], dzr[:, HD:])).astype(BF16)
    kc[512:1024, :] = regroup(mm(xq[0:512, :], dzr[:, 0:HD])).astype(BF16)
    c2 = put(kc, kcr, 7, at(dc=1))
    c2.start()
    cb[...] = (cpre[0, 0:512, :] * va + cpre[1, 0:512, :] * vc).astype(BF16)
    c1 = put(cb, cr, 6, at(dc=1))
    c1.start()
    kown[0:512, :] = regroup(mm(xz[512:1024, :], dzr[:, HD:]))
    kown[512:1024, :] = regroup(mm(xq[512:1024, :], dzr[:, 0:HD]))
    c2.wait_recv()
    for k in RING:
        for p, i, axis in ((0, 9, "dy"), (1, 12, "dz_")):
            a = slice(p * 512 + k * 64, p * 512 + k * 64 + 64)
            kb[p, k] = (kown[a, :] + kcr[a, :].astype(F32)).astype(BF16)
            put(kb.at[p, k], kr.at[p, k], i, at(**{axis: k})).start()
    own[...] = cpre[0, 512:1024, :] * va + cpre[1, 512:1024, :] * vc
    c1.wait_recv()
    for k in (2, 1, 3):
        a = slice(k * 128, (k + 1) * 128)
        xb[k] = (own[a, :] + cr[a, :].astype(F32)).astype(BF16)
        put(xb.at[k], xr.at[k], 8, at(dx=k)).start()

    whole(gys.at[0], gyr.at[0], 5, "dy").wait_recv()
    whole(gys.at[1], gyr.at[1], 16, "dz_").wait_recv()
    g = jnp.concatenate([mine[p] + jnp.sum(gyr[p, 1:8].astype(F32), axis=0) for p in range(2)], axis=1)
    gp = mm(jnp.concatenate([g, jnp.zeros((6, D), F32)], axis=0).astype(BF16), pz[...], NT)
    m2 = jnp.concatenate([mvec[0, 0:1, :], mvec[1, 0:1, :]], axis=0)
    for dc in range(2):
        for dx in range(4):
            q = (1 - dc) * 4 + dx
            gm[dc * 4 + dx, 0:2, :] = gp[0:2, q * HD : (q + 1) * HD]
            gm[dc * 4 + dx, 2:4, :] = m2
    for k in (6, 2, 5, 7, 1, 3, 4):
        put(gm.at[k], gmr.at[k], 10, at(dc=k // 4, dx=k % 4)).start()
    gmr[0] = gm[0]

    def back(h, carry):
        n, inv, keep = shares(h)
        hr = pl.ds(pl.multiple_of(h * L, L), L)
        vh = jnp.where(h == 0, va, vc)
        dz[hr, 0 : 2 * HD] = (pre[h] * vh).astype(BF16)
        dn = mm(dz[hr, :], wi[...], NT)
        r = rs[h, :, 0:1]
        xn = hist[h].astype(F32) * r
        mean = jnp.sum(dn * xn, axis=1, keepdims=True) * (1.0 / D)
        gh = jnp.where(h == 0, g[0:1, :], g[1:2, :])
        dx_o[h] = (r * (dn - xn * mean) + keep * gh).astype(BF16)
        return carry

    lax.fori_loop(0, 1, back, 0)

    whole(xb, xr, 8, "dx").wait_recv()
    t0 = own[0:128, :] + cr[0:128, :].astype(F32)
    for k in range(1, 4):
        t0 = t0 + xr[k].astype(F32)
    put(gm.at[1:8], gmr.at[1:8], 10, at(dc=1)).wait_recv()
    gx = jnp.concatenate([gmr[k, 0:2, :] for k in range(8)], axis=0)
    mx = jnp.concatenate([gmr[k, 2:4, :] for k in range(8)], axis=0)
    so = mm(gx.astype(BF16), mx.astype(BF16), TN)
    t = jnp.concatenate([t0, so], axis=1)
    fbt[...] = t.astype(BF16)
    for a in RING + (0,):
        for b in RING + (0,):
            k = a * 8 + b
            if k:
                fb[k] = fbt[2 * k : 2 * k + 2, :]
                put(fb.at[k], fr.at[k], 11, at(dy=a, dz_=b)).start()

    lax.fori_loop(1, 2, back, 0)

    tk = []
    for p, i, axis in ((0, 9, "dy"), (1, 12, "dz_")):
        whole(kb.at[p], kr.at[p], i, axis).wait_recv()
        a = slice(p * 512, p * 512 + 64)
        q = kown[a, :] + kcr[a, :].astype(F32)
        for k in range(1, 8):
            q = q + kr[p, k].astype(F32)
        tk.append(q[0:2])
        for a in (2, 1, 3, 0):
            for b in RING + (0,):
                k = a * 8 + b
                if k:
                    kf[p, k] = q[2 * k : 2 * k + 2]
                    other = {"dx": a, ("dy", "dz_")[1 - p]: b}
                    put(kf.at[p, k], kfr.at[p, k], 13 + p, at(**other)).start()

    @pl.when(c == 0)
    def _():
        put(tvb, tvb, 0, at(dc=1)).wait_send()

    @pl.when(c == 1)
    def _():
        put(tvb.at[32:256], tvb.at[32:256], 0, at(dc=1)).wait_send()
        whole(vys, vyr, 2, "dy").wait_send()
        v_core.wait_send()

    for cp in (g_core, c1, c2):
        cp.wait_send()
    whole(ub, gzr, 3, "dz_", 16).wait_send()
    whole(ub.at[128:256], gzr.at[128:256], 15, "dy", 16).wait_send()
    whole(gys.at[0], gyr.at[0], 5, "dy").wait_send()
    whole(gys.at[1], gyr.at[1], 16, "dz_").wait_send()
    whole(xb, xr, 8, "dx").wait_send()
    whole(kb.at[0], kr.at[0], 9, "dy").wait_send()
    whole(kb.at[1], kr.at[1], 12, "dz_").wait_send()
    put(gm.at[1:8], gmr.at[1:8], 10, at(dc=1)).wait_send()

    put(fb.at[1:64], fr.at[1:64], 11, at(dy=1)).wait()
    f = t[0:2, :] + jnp.sum(fr[1:64].astype(F32), axis=0)
    gin_o[:, 0:256] = f[:, 0:256]
    gout_o[...] = f[:, 256:384]
    for p, cols in ((1, slice(256, 384)), (0, slice(384, 512))):
        put(kf.at[p, 1:32], kfr.at[p, 1:32], 13 + p, at(dx=1)).wait()
        gin_o[:, cols] = tk[p] + jnp.sum(kfr[p, 1:32], axis=0)


def finish(dx_v, gin_v, gout_v, dx_o, gin_o, gout_o, sem):
    pairs = [(dx_v.at[h, r : r + 128], dx_o.at[h, r : r + 128]) for h in range(2) for r in (0, 128)]
    pairs += [(gin_v, gin_o), (gout_v, gout_o)]
    copies = [pltpu.make_async_copy(a, b, sem.at[i]) for i, (a, b) in enumerate(pairs)]
    for copy in copies:
        copy.start()
    for copy in copies:
        copy.wait()


def body(sample_grads, send_count, send_user, histories, hist_len, w_in, w_out):
    vm = pl.BlockSpec(memory_space=pltpu.VMEM)
    hbm = pl.BlockSpec(memory_space=pl.ANY)
    V = pltpu.VMEM
    sd = jax.ShapeDtypeStruct
    dx, gin, gout = pl.pallas_call(
        kernel,
        out_shape=(V((2, L, D), BF16), V((2, 512), F32), V((2, HD), F32)),
        in_specs=[pl.BlockSpec(memory_space=pltpu.SMEM), hbm, hbm, hbm, hbm, hbm, hbm],
        out_specs=(vm, vm, vm),
        scratch_shapes=[
            V((1, 128), I32), V((4, 128), I32), V((256, D), BF16), V((2, L, D), BF16), V((D, 512), BF16), V((HD, D), BF16),
            V((256, HD), F32), V((256, HD), BF16), V((480, HD), BF16), V((8, 4, HD), F32), V((8, 4, HD), F32), V((4, HD), F32),
            V((256, 512), BF16), V((256, 512), BF16), V((256, 512), F32), V((256, 512), BF16), V((256, 512), BF16),
            V((2, 8, 2, 512), BF16), V((2, 8, 2, 512), BF16),
            V((D, D), BF16), V((D, 512), BF16), V((D, 512), BF16),
            V((2, L, HD), F32), V((2, L, 256), F32), V((2, L, 256), BF16), V((2, L, L), BF16), V((2, L, L), F32),
            V((2, L, 3 * HD), BF16), V((2, L, 256), F32), V((2, L, HD), F32),
            V((512, 512), BF16), V((512, 256), BF16), V((2, 8, HD), F32), V((2, D, 256), F32),
            V((512, 256), BF16), V((512, 256), BF16), V((512, 256), F32),
            V((1024, HD), BF16), V((1024, HD), BF16), V((1024, HD), F32),
            V((4, 128, 256), BF16), V((4, 128, 256), BF16), V((2, 8, 64, HD), BF16), V((2, 8, 64, HD), BF16),
            V((8, 4, HD), F32), V((8, 4, HD), F32), V((128, 384), BF16), V((64, 2, 384), BF16), V((64, 2, 384), BF16),
            V((2, 32, 2, HD), F32), V((2, 32, 2, HD), F32),
            pltpu.SemaphoreType.DMA((6,)), pltpu.SemaphoreType.DMA((17,)), pltpu.SemaphoreType.DMA((17,)),
        ],
        compiler_params=pltpu.CompilerParams(
            collective_id=0, has_side_effects=True, vmem_limit_bytes=VMEM
        ),
        name="encoder_backward",
    )(hist_len, send_count, send_user.T, sample_grads, histories, w_in, w_out)
    dx, gin, gout = pl.pallas_call(
        finish,
        out_shape=(sd((2, L, D), BF16), sd((2, 512), F32), sd((2, HD), F32)),
        in_specs=[vm, vm, vm],
        out_specs=(hbm, hbm, hbm),
        scratch_shapes=[pltpu.SemaphoreType.DMA((6,))],
        compiler_params=pltpu.CompilerParams(vmem_limit_bytes=8 * 1024 * 1024),
        name="finish",
    )(dx, gin, gout)
    return dx, gin, gout.T


def solution(mesh):
    both = ("own", "rep")
    return jax.shard_map(
        body,
        mesh=mesh,
        in_specs=(P(both, None), P(both, None), P(both, None), P(both, None, None), P(both), P(), P()),
        out_specs=(P(both, None, None), P(both, None), P(None, both)),
        check_vma=False,
    )
```

```python
import jax
import jax.numpy as jnp
from jax import lax
from jax.experimental import pallas as pl
from jax.experimental.pallas import tpu as pltpu
from jax.sharding import PartitionSpec as P

MESH = pl.DeviceIdType.MESH
F32, BF16, I32 = jnp.float32, jnp.bfloat16, jnp.int32
D, HD, L = 1024, 128, 256
VMEM = 61 * 1024 * 1024
RING = (4, 3, 5, 2, 6, 1, 7)
NT = (((1,), (1,)), ((), ()))
TN = (((0,), (0,)), ((), ()))


def mm(a, b, dims=(((1,), (0,)), ((), ()))):
    return lax.dot_general(a, b, dims, preferred_element_type=F32)


def kernel(
    len_s, cnt_h, slot_h, sg_h, hist_h, wi_h, wo_h,
    dx_o, gin_o, gout_o,
    cnt_v, slot_v, sg, hist, wi, wo,
    tv, tvb, vzr, vys, vyr, vfin,
    tb, tr, ua, ub, gzr, gys, gyr,
    pz, xz, xq,
    kgate, pre, preg, wgt, dsw, pj, dsl, rs, dz, dzr, mvec, cpre,
    cb, cr, own, kc, kcr, kown, xb, xr, kb, kr, gm, gmr, fbt, fb, fr, kf, kfr,
    load, send, recv,
):
    o_id = lax.axis_index("own")
    x = lax.axis_index("rep")
    y, z, c = o_id // 16, (o_id // 2) % 8, o_id % 2

    def at(dy=0, dz_=0, dc=0, dx=0, core=None):
        k = lax.rem(c + dc, 2) if core is None else core
        return (lax.rem(y + dy, 8) * 8 + lax.rem(z + dz_, 8)) * 2 + k, lax.rem(x + dx, 4)

    def put(src, dst, i, dev):
        return pltpu.make_async_remote_copy(
            src_ref=src, dst_ref=dst, send_sem=send.at[i], recv_sem=recv.at[i], device_id=dev, device_id_type=MESH
        )

    def many(src, dst, i, axis, rows=None):
        for k in (2, 1, 3) if axis == "dx" else RING:
            a = k if rows is None else slice(rows * k, rows * k + rows)
            put(src.at[a], dst.at[a], i, at(**{axis: k})).start()

    def whole(src, dst, i, axis, rows=None):
        n = 4 if axis == "dx" else 8
        a = slice(1, n) if rows is None else slice(rows, rows * n)
        return put(src.at[a], dst.at[a], i, at(**{axis: 1}))

    barrier = pltpu.get_barrier_semaphore()
    peers = [at(dc=1)] + [at(dy=k) for k in RING] + [at(dz_=k) for k in RING] + [at(dx=k) for k in (2, 1, 3)]
    for dev in peers:
        pl.semaphore_signal(barrier, 1, device_id=dev, device_id_type=MESH)

    @pl.when(c == 1)
    def _():
        for k in RING:
            pl.semaphore_signal(barrier, 1, device_id=at(dz_=k, core=0), device_id_type=MESH)

    def fetch(i, src, dst):
        cp = pltpu.make_async_copy(src, dst, load.at[i])
        cp.start()
        return cp

    small = [fetch(0, cnt_h, cnt_v), fetch(1, slot_h, slot_v)]
    for k in range(0, 256, 64):
        pltpu.make_async_copy(sg_h.at[k : k + 64], sg.at[k : k + 64], load.at[2]).start()
    small += [pltpu.make_async_copy(sg_h, sg, load.at[2]), fetch(3, wo_h, wo)]
    large = [fetch(4, hist_h, hist), fetch(5, wi_h, wi)]

    ri = lax.broadcasted_iota(I32, (256, 1), 0)
    lane = lax.broadcasted_iota(I32, (256, 128), 1)
    samp = lax.broadcasted_iota(I32, (256, 256), 1).astype(F32)
    user = lax.rem(ri, 2).astype(F32)
    for cp in small[:2]:
        cp.wait()
    cnt = cnt_v[...].astype(F32)
    slots = slot_v[...].astype(F32).astype(BF16)

    def onehot(ry_, rz_, core):
        oi = (lax.rem(y + ry_, 8) * 8 + lax.rem(z + rz_, 8)) * 2 + core
        off = jnp.sum(jnp.where(lane < oi, cnt, 0.0), axis=1, keepdims=True)
        num = jnp.sum(jnp.where(lane == oi, cnt, 0.0), axis=1, keepdims=True)
        su = mm((lane == oi).astype(F32).astype(BF16), slots, NT)
        d = samp - off
        hit = jnp.zeros((256, 256), F32)
        for k in range(4):
            live = jnp.where((num > k) & (su[:, k : k + 1] == user), 1.0, 0.0)
            hit = hit + jnp.where(d == k, live, 0.0)
        return hit.astype(BF16)

    hit = onehot(lax.rem(ri // 4, 8), ri // 32, lax.rem(ri // 2, 2))
    for cp in small[2:]:
        cp.wait()
    tv[...] = mm(hit, mm(sg[...], wo[...], NT).astype(BF16))
    tvb[...] = tv[...].astype(BF16)

    def vput(k):
        slot = pl.ds(pl.multiple_of((k + 7 * c) * 32, 32), 32)
        return put(tvb.at[32 * k : 32 * k + 32], vzr.at[slot], 0, at(dz_=k, core=1))

    pl.semaphore_wait(barrier, len(peers) + 7 * (1 - c))
    for k in RING:
        vput(k).start()

    @pl.when(c == 0)
    def _():
        put(tvb.at[0:32], vzr.at[0:32], 0, at(dc=1)).start()

    hit = onehot(lax.rem(ri // 2, 8), lax.rem(ri // 16, 8), lax.rem(c + 1 - ri // 128 + 2, 2))
    sr = lax.broadcasted_iota(I32, (128, 1), 0)
    sl = lax.broadcasted_iota(I32, (128, 128), 1)
    swap = (sl == lax.rem(sr // 2, 8) * 16 + sr // 16 * 2 + lax.rem(sr, 2)).astype(F32).astype(BF16)
    other = jnp.concatenate([mm(swap, hit[0:128]), mm(swap, hit[128:256])], axis=0).astype(BF16)
    tb[0:128, :] = mm(hit[0:128], sg[:, 0:512]).astype(BF16)
    tb[128:256, :] = mm(other[0:128], sg[:, 512:]).astype(BF16)
    g_core = put(tb, tr, 1, at(dc=1))
    g_core.start()
    ua[0:128, :] = mm(hit[128:256], sg[:, 0:512])
    ua[128:256, :] = mm(other[128:256], sg[:, 512:])

    for cp in large:
        cp.wait()
    ti = lax.broadcasted_iota(I32, (L, 1), 0)
    tj = lax.broadcasted_iota(I32, (L, L), 1)

    def shares(h):
        n = len_s[h]
        inv = 1.0 / jnp.full((1, 1), n, I32).astype(F32)
        return n, inv, jnp.where(ti < n, 1.0, 0.0) * inv

    def forward(h, carry):
        n, inv, keep = shares(h)
        xf = hist[h].astype(F32)
        r = lax.rsqrt(jnp.sum(xf * xf, axis=1, keepdims=True) * (1.0 / D) + 1e-05)
        rs[h] = jnp.broadcast_to(r, (L, HD))
        zz = mm((xf * r).astype(BF16), wi[...])
        sig = 1.0 / (1.0 + jnp.exp(-zz))
        p = zz * sig
        ds = sig + p * (1.0 - sig)
        dsl[h] = ds[:, 2 * HD :]
        pj[h] = p[:, HD:].astype(BF16)
        s = mm(pj[h, :, HD : 2 * HD], pj[h, :, 2 * HD :], NT) * HD**-0.5
        vis = (tj <= ti) & (tj < n)
        ss = 1.0 / (1.0 + jnp.exp(-s))
        sw = s * ss
        wgt[h] = (jnp.where(vis, sw, 0.0) * inv).astype(BF16)
        dsw[h] = jnp.where(vis, ss + sw * (1.0 - ss), 0.0) * (inv * HD**-0.5)
        att = mm(wgt[h], pj[h, :, 0:HD])
        mixed = (att * p[:, 0:HD]).astype(BF16).astype(F32)
        mvec[h] = jnp.broadcast_to(jnp.sum(mixed * keep, axis=0, keepdims=True), (8, HD))
        kg = keep * p[:, 0:HD]
        kgate[h] = kg
        pg = keep * att * ds[:, 0:HD]
        pv = mm(wgt[h], kg.astype(BF16), TN) * ds[:, HD : 2 * HD]
        pre[h, :, 0:HD] = pg
        pre[h, :, HD:] = pv
        preg[h, :, 0:HD] = (pg * r).astype(BF16)
        preg[h, :, HD:] = (pv * r).astype(BF16)
        return carry

    lax.fori_loop(0, 1, forward, 0)
    g_core.wait_recv()
    ua[...] = ua[...] + tr[...].astype(F32)
    ub[...] = ua[...].astype(BF16)
    many(ub, gzr, 3, "dz_", 16)
    many(ub.at[128:256], gzr.at[128:256], 15, "dy", 16)
    lax.fori_loop(1, 2, forward, 0)


    @pl.when(c == 1)
    def _():
        put(vzr.at[0:480], vzr.at[0:480], 0, at(dc=1)).wait_recv()
        s = tv[0:32, :]
        for k in range(15):
            s = s + vzr[32 * k : 32 * k + 32, :].astype(F32)
        for k in range(8):
            vys[k] = s[4 * k : 4 * k + 4]
        many(vys, vyr, 2, "dy")
        vyr[0] = s[0:4]

    pr = lax.broadcasted_iota(I32, (512, 1), 0)
    fl = lax.broadcasted_iota(I32, (512, D), 1)

    def permute(i, carry):
        r = pr + i * 512
        crel, xrel, ry_, rz_, j = r // 512, lax.rem(r // 128, 4), lax.rem(r // 16, 8), lax.rem(r // 2, 8), lax.rem(r, 2)
        f = (lax.rem(y + ry_, 8) * 8 + lax.rem(z + rz_, 8)) * 2 + lax.rem(c + 1 - crel + 2, 2)
        f = f * 8 + lax.rem(x + xrel, 4) * 2 + j
        rows = pl.ds(pl.multiple_of(i * 512, 512), 512)
        pm = (fl == f).astype(F32).astype(BF16)
        pz[rows, :] = pm
        xz[rows, :] = mm(pm, hist[...].reshape(2 * L, D), NT).astype(BF16)
        for h in range(2):
            cpre[h, rows, :] = mm(xz[rows, h * L : (h + 1) * L], preg[h])
        return carry

    lax.fori_loop(0, 2, permute, 0)
    for k in range(0, D, 128):
        xq[k : k + 128, :] = mm(swap, xz[k : k + 128, :]).astype(BF16)

    whole(ub, gzr, 3, "dz_", 16).wait_recv()
    whole(ub.at[128:256], gzr.at[128:256], 15, "dy", 16).wait_recv()
    mine = []
    for p, i, axis in ((0, 5, "dy"), (1, 16, "dz_")):
        s1 = ua[128 * p : 128 * p + 16, :]
        for k in range(1, 8):
            s1 = s1 + gzr[128 * p + 16 * k : 128 * p + 16 * k + 16, :].astype(F32)
        mine.append(s1[0:2])
        s1 = s1.astype(BF16)
        for k in range(1, 8):
            gys[p, k] = s1[2 * k : 2 * k + 2]
        many(gys.at[p], gyr.at[p], i, axis)

    v_core = put(vfin, vfin, 4, at(dc=1))

    @pl.when(c == 1)
    def _():
        whole(vys, vyr, 2, "dy").wait_recv()
        vfin[...] = jnp.sum(vyr[...], axis=0)
        v_core.start()

    @pl.when(c == 0)
    def _():
        v_core.wait_recv()

    v = jnp.where(c == 0, vfin[0:2, :], vfin[2:4, :])
    va = jnp.concatenate([v[0:1], v[0:1]], axis=1)
    vc = jnp.concatenate([v[1:2], v[1:2]], axis=1)
    cb[...] = (cpre[0, 0:512, :] * va + cpre[1, 0:512, :] * vc).astype(BF16)
    c1 = put(cb, cr, 6, at(dc=1))
    c1.start()
    for h in range(2):
        datt = (kgate[h] * v[h : h + 1, :]).astype(BF16)
        ds = (mm(datt, pj[h, :, 0:HD], NT) * dsw[h]).astype(BF16)
        dq = mm(ds, pj[h, :, 2 * HD :])
        dk = mm(ds, pj[h, :, HD : 2 * HD], TN)
        hr = slice(h * L, (h + 1) * L)
        for i, part in enumerate((dq, dk)):
            full = part * dsl[h, :, i * HD : (i + 1) * HD]
            dz[hr, (i + 2) * HD : (i + 3) * HD] = full.astype(BF16)
            dzr[hr, i * HD : (i + 1) * HD] = (full * rs[h]).astype(BF16)

    def regroup(r):
        return jnp.concatenate([r[a * 128 + b * 16 : a * 128 + b * 16 + 16] for b in range(8) for a in range(4)], axis=0)

    kc[0:512, :] = regroup(mm(xz[0:512, :], dzr[:, HD:])).astype(BF16)
    kc[512:1024, :] = regroup(mm(xq[0:512, :], dzr[:, 0:HD])).astype(BF16)
    c2 = put(kc, kcr, 7, at(dc=1))
    c2.start()
    own[...] = cpre[0, 512:1024, :] * va + cpre[1, 512:1024, :] * vc
    c1.wait_recv()
    for k in (2, 1, 3):
        a = slice(k * 128, (k + 1) * 128)
        xb[k] = (own[a, :] + cr[a, :].astype(F32)).astype(BF16)
        put(xb.at[k], xr.at[k], 8, at(dx=k)).start()
    kown[0:512, :] = regroup(mm(xz[512:1024, :], dzr[:, HD:]))
    kown[512:1024, :] = regroup(mm(xq[512:1024, :], dzr[:, 0:HD]))
    c2.wait_recv()
    for k in RING:
        for p, i, axis in ((0, 9, "dy"), (1, 12, "dz_")):
            a = slice(p * 512 + k * 64, p * 512 + k * 64 + 64)
            kb[p, k] = (kown[a, :] + kcr[a, :].astype(F32)).astype(BF16)
            put(kb.at[p, k], kr.at[p, k], i, at(**{axis: k})).start()

    whole(gys.at[0], gyr.at[0], 5, "dy").wait_recv()
    whole(gys.at[1], gyr.at[1], 16, "dz_").wait_recv()
    g = jnp.concatenate([mine[p] + jnp.sum(gyr[p, 1:8].astype(F32), axis=0) for p in range(2)], axis=1)
    gp = mm(jnp.concatenate([g, jnp.zeros((6, D), F32)], axis=0).astype(BF16), pz[...], NT)
    m2 = jnp.concatenate([mvec[0, 0:1, :], mvec[1, 0:1, :]], axis=0)
    for dc in range(2):
        for dx in range(4):
            q = (1 - dc) * 4 + dx
            gm[dc * 4 + dx, 0:2, :] = gp[0:2, q * HD : (q + 1) * HD]
            gm[dc * 4 + dx, 2:4, :] = m2
    for k in (6, 2, 5, 7, 1, 3, 4):
        put(gm.at[k], gmr.at[k], 10, at(dc=k // 4, dx=k % 4)).start()
    gmr[0] = gm[0]

    def back(h, carry):
        n, inv, keep = shares(h)
        hr = pl.ds(pl.multiple_of(h * L, L), L)
        vh = jnp.where(h == 0, va, vc)
        dz[hr, 0 : 2 * HD] = (pre[h] * vh).astype(BF16)
        dn = mm(dz[hr, :], wi[...], NT)
        r = rs[h, :, 0:1]
        xn = hist[h].astype(F32) * r
        mean = jnp.sum(dn * xn, axis=1, keepdims=True) * (1.0 / D)
        gh = jnp.where(h == 0, g[0:1, :], g[1:2, :])
        dx_o[h] = (r * (dn - xn * mean) + keep * gh).astype(BF16)
        return carry

    lax.fori_loop(0, 1, back, 0)

    whole(xb, xr, 8, "dx").wait_recv()
    t0 = own[0:128, :] + cr[0:128, :].astype(F32)
    for k in range(1, 4):
        t0 = t0 + xr[k].astype(F32)
    put(gm.at[1:8], gmr.at[1:8], 10, at(dc=1)).wait_recv()
    gx = jnp.concatenate([gmr[k, 0:2, :] for k in range(8)], axis=0)
    mx = jnp.concatenate([gmr[k, 2:4, :] for k in range(8)], axis=0)
    so = mm(gx.astype(BF16), mx.astype(BF16), TN)
    t = jnp.concatenate([t0, so], axis=1)
    fbt[...] = t.astype(BF16)
    for a in RING + (0,):
        for b in RING + (0,):
            k = a * 8 + b
            if k:
                fb[k] = fbt[2 * k : 2 * k + 2, :]
                put(fb.at[k], fr.at[k], 11, at(dy=a, dz_=b)).start()

    lax.fori_loop(1, 2, back, 0)

    tk = []
    for p, i, axis in ((0, 9, "dy"), (1, 12, "dz_")):
        whole(kb.at[p], kr.at[p], i, axis).wait_recv()
        a = slice(p * 512, p * 512 + 64)
        q = kown[a, :] + kcr[a, :].astype(F32)
        for k in range(1, 8):
            q = q + kr[p, k].astype(F32)
        tk.append(q[0:2])
        for a in (2, 1, 3, 0):
            for b in RING + (0,):
                k = a * 8 + b
                if k:
                    kf[p, k] = q[2 * k : 2 * k + 2]
                    other = {"dx": a, ("dy", "dz_")[1 - p]: b}
                    put(kf.at[p, k], kfr.at[p, k], 13 + p, at(**other)).start()

    @pl.when(c == 0)
    def _():
        put(tvb, tvb, 0, at(dc=1)).wait_send()

    @pl.when(c == 1)
    def _():
        put(tvb.at[32:256], tvb.at[32:256], 0, at(dc=1)).wait_send()
        whole(vys, vyr, 2, "dy").wait_send()
        v_core.wait_send()

    for cp in (g_core, c1, c2):
        cp.wait_send()
    whole(ub, gzr, 3, "dz_", 16).wait_send()
    whole(ub.at[128:256], gzr.at[128:256], 15, "dy", 16).wait_send()
    whole(gys.at[0], gyr.at[0], 5, "dy").wait_send()
    whole(gys.at[1], gyr.at[1], 16, "dz_").wait_send()
    whole(xb, xr, 8, "dx").wait_send()
    whole(kb.at[0], kr.at[0], 9, "dy").wait_send()
    whole(kb.at[1], kr.at[1], 12, "dz_").wait_send()
    put(gm.at[1:8], gmr.at[1:8], 10, at(dc=1)).wait_send()

    put(fb.at[1:64], fr.at[1:64], 11, at(dy=1)).wait()
    f = t[0:2, :] + jnp.sum(fr[1:64].astype(F32), axis=0)
    gin_o[:, 0:256] = f[:, 0:256]
    gout_o[...] = f[:, 256:384]
    for p, cols in ((1, slice(256, 384)), (0, slice(384, 512))):
        put(kf.at[p, 1:32], kfr.at[p, 1:32], 13 + p, at(dx=1)).wait()
        gin_o[:, cols] = tk[p] + jnp.sum(kfr[p, 1:32], axis=0)


def finish(dx_v, gin_v, gout_v, dx_o, gin_o, gout_o, sem):
    pairs = [(dx_v.at[h, r : r + 128], dx_o.at[h, r : r + 128]) for h in range(2) for r in (0, 128)]
    pairs += [(gin_v, gin_o), (gout_v, gout_o)]
    copies = [pltpu.make_async_copy(a, b, sem.at[i]) for i, (a, b) in enumerate(pairs)]
    for copy in copies:
        copy.start()
    for copy in copies:
        copy.wait()


def body(sample_grads, send_count, send_user, histories, hist_len, w_in, w_out):
    vm = pl.BlockSpec(memory_space=pltpu.VMEM)
    hbm = pl.BlockSpec(memory_space=pl.ANY)
    V = pltpu.VMEM
    sd = jax.ShapeDtypeStruct
    dx, gin, gout = pl.pallas_call(
        kernel,
        out_shape=(V((2, L, D), BF16), V((2, 512), F32), V((2, HD), F32)),
        in_specs=[pl.BlockSpec(memory_space=pltpu.SMEM), hbm, hbm, hbm, hbm, hbm, hbm],
        out_specs=(vm, vm, vm),
        scratch_shapes=[
            V((1, 128), I32), V((4, 128), I32), V((256, D), BF16), V((2, L, D), BF16), V((D, 512), BF16), V((HD, D), BF16),
            V((256, HD), F32), V((256, HD), BF16), V((480, HD), BF16), V((8, 4, HD), F32), V((8, 4, HD), F32), V((4, HD), F32),
            V((256, 512), BF16), V((256, 512), BF16), V((256, 512), F32), V((256, 512), BF16), V((256, 512), BF16),
            V((2, 8, 2, 512), BF16), V((2, 8, 2, 512), BF16),
            V((D, D), BF16), V((D, 512), BF16), V((D, 512), BF16),
            V((2, L, HD), F32), V((2, L, 256), F32), V((2, L, 256), BF16), V((2, L, L), BF16), V((2, L, L), F32),
            V((2, L, 3 * HD), BF16), V((2, L, 256), F32), V((2, L, HD), F32),
            V((512, 512), BF16), V((512, 256), BF16), V((2, 8, HD), F32), V((2, D, 256), F32),
            V((512, 256), BF16), V((512, 256), BF16), V((512, 256), F32),
            V((1024, HD), BF16), V((1024, HD), BF16), V((1024, HD), F32),
            V((4, 128, 256), BF16), V((4, 128, 256), BF16), V((2, 8, 64, HD), BF16), V((2, 8, 64, HD), BF16),
            V((8, 4, HD), F32), V((8, 4, HD), F32), V((128, 384), BF16), V((64, 2, 384), BF16), V((64, 2, 384), BF16),
            V((2, 32, 2, HD), F32), V((2, 32, 2, HD), F32),
            pltpu.SemaphoreType.DMA((6,)), pltpu.SemaphoreType.DMA((17,)), pltpu.SemaphoreType.DMA((17,)),
        ],
        compiler_params=pltpu.CompilerParams(
            collective_id=0, has_side_effects=True, vmem_limit_bytes=VMEM
        ),
        name="encoder_backward",
    )(hist_len, send_count, send_user.T, sample_grads, histories, w_in, w_out)
    dx, gin, gout = pl.pallas_call(
        finish,
        out_shape=(sd((2, L, D), BF16), sd((2, 512), F32), sd((2, HD), F32)),
        in_specs=[vm, vm, vm],
        out_specs=(hbm, hbm, hbm),
        scratch_shapes=[pltpu.SemaphoreType.DMA((6,))],
        compiler_params=pltpu.CompilerParams(vmem_limit_bytes=8 * 1024 * 1024),
        name="finish",
    )(dx, gin, gout)
    return dx, gin, gout.T


def solution(mesh):
    both = ("own", "rep")
    return jax.shard_map(
        body,
        mesh=mesh,
        in_specs=(P(both, None), P(both, None), P(both, None), P(both, None, None), P(both), P(), P()),
        out_specs=(P(both, None, None), P(both, None), P(None, both)),
        check_vma=False,
    )
```

```python
import jax
import jax.numpy as jnp
from jax import lax
from jax.experimental import pallas as pl
from jax.experimental.pallas import tpu as pltpu
from jax.sharding import PartitionSpec as P

MESH = pl.DeviceIdType.MESH
F32, BF16, I32 = jnp.float32, jnp.bfloat16, jnp.int32
D, HD, L = 1024, 128, 256
VMEM = 61 * 1024 * 1024
RING = (4, 3, 5, 2, 6, 1, 7)
NT = (((1,), (1,)), ((), ()))
TN = (((0,), (0,)), ((), ()))


def mm(a, b, dims=(((1,), (0,)), ((), ()))):
    return lax.dot_general(a, b, dims, preferred_element_type=F32)


def kernel(
    len_s, cnt_h, slot_h, sg_h, hist_h, wi_h, wo_h,
    dx_o, gin_o, gout_o,
    cnt_v, slot_v, sg, hist, wi, wo,
    tv, tvb, vzr, vys, vyr,
    tb, tr, ua, ub, gzr, gys, gyr,
    pz, xz, xq,
    kgate, pre, preg, wgt, dsw, pj, dsl, rs, dz, dzr, mvec, cpre,
    cb, cr, own, kc, kcr, kown, xb, xr, kb, kr, gm, gmr, fbt, fb, fr, kf, kfr,
    load, send, recv,
):
    o_id = lax.axis_index("own")
    x = lax.axis_index("rep")
    y, z, c = o_id // 16, (o_id // 2) % 8, o_id % 2

    def at(dy=0, dz_=0, dc=0, dx=0, core=None):
        k = lax.rem(c + dc, 2) if core is None else core
        return (lax.rem(y + dy, 8) * 8 + lax.rem(z + dz_, 8)) * 2 + k, lax.rem(x + dx, 4)

    def put(src, dst, i, dev):
        return pltpu.make_async_remote_copy(
            src_ref=src, dst_ref=dst, send_sem=send.at[i], recv_sem=recv.at[i], device_id=dev, device_id_type=MESH
        )

    def many(src, dst, i, axis, rows=None):
        for k in (2, 1, 3) if axis == "dx" else RING:
            a = k if rows is None else slice(rows * k, rows * k + rows)
            put(src.at[a], dst.at[a], i, at(**{axis: k})).start()

    def whole(src, dst, i, axis, rows=None):
        n = 4 if axis == "dx" else 8
        a = slice(1, n) if rows is None else slice(rows, rows * n)
        return put(src.at[a], dst.at[a], i, at(**{axis: 1}))

    barrier = pltpu.get_barrier_semaphore()
    peers = [at(dc=1)] + [at(dy=k) for k in RING] + [at(dz_=k) for k in RING] + [at(dx=k) for k in (2, 1, 3)]
    for dev in peers:
        pl.semaphore_signal(barrier, 1, device_id=dev, device_id_type=MESH)

    @pl.when(c == 1)
    def _():
        for k in RING:
            pl.semaphore_signal(barrier, 1, device_id=at(dz_=k, core=0), device_id_type=MESH)

    @pl.when(c == 0)
    def _():
        for k in RING:
            pl.semaphore_signal(barrier, 1, device_id=at(dy=k, core=1), device_id_type=MESH)

    def fetch(i, src, dst):
        cp = pltpu.make_async_copy(src, dst, load.at[i])
        cp.start()
        return cp

    small = [fetch(0, cnt_h, cnt_v), fetch(1, slot_h, slot_v)]
    for k in range(0, 256, 64):
        pltpu.make_async_copy(sg_h.at[k : k + 64], sg.at[k : k + 64], load.at[2]).start()
    small += [pltpu.make_async_copy(sg_h, sg, load.at[2]), fetch(3, wo_h, wo)]
    large = [fetch(4, hist_h, hist), fetch(5, wi_h, wi)]

    ri = lax.broadcasted_iota(I32, (256, 1), 0)
    lane = lax.broadcasted_iota(I32, (256, 128), 1)
    samp = lax.broadcasted_iota(I32, (256, 256), 1).astype(F32)
    user = lax.rem(ri, 2).astype(F32)
    for cp in small[:2]:
        cp.wait()
    cnt = cnt_v[...].astype(F32)
    slots = slot_v[...].astype(F32).astype(BF16)

    def onehot(ry_, rz_, core):
        oi = (lax.rem(y + ry_, 8) * 8 + lax.rem(z + rz_, 8)) * 2 + core
        off = jnp.sum(jnp.where(lane < oi, cnt, 0.0), axis=1, keepdims=True)
        num = jnp.sum(jnp.where(lane == oi, cnt, 0.0), axis=1, keepdims=True)
        su = mm((lane == oi).astype(F32).astype(BF16), slots, NT)
        d = samp - off
        hit = jnp.zeros((256, 256), F32)
        for k in range(4):
            live = jnp.where((num > k) & (su[:, k : k + 1] == user), 1.0, 0.0)
            hit = hit + jnp.where(d == k, live, 0.0)
        return hit.astype(BF16)

    hit = onehot(lax.rem(ri // 4, 8), ri // 32, lax.rem(ri // 2, 2))
    for cp in small[2:]:
        cp.wait()
    tv[...] = mm(hit, mm(sg[...], wo[...], NT).astype(BF16))
    tvb[...] = tv[...].astype(BF16)

    def vput(k):
        slot = pl.ds(pl.multiple_of((k + 7 * c) * 32, 32), 32)
        return put(tvb.at[32 * k : 32 * k + 32], vzr.at[slot], 0, at(dz_=k, core=1))

    pl.semaphore_wait(barrier, len(peers) + 7)
    for k in RING:
        vput(k).start()

    @pl.when(c == 0)
    def _():
        put(tvb.at[0:32], vzr.at[0:32], 0, at(dc=1)).start()

    hit = onehot(lax.rem(ri // 2, 8), lax.rem(ri // 16, 8), lax.rem(c + 1 - ri // 128 + 2, 2))
    sr = lax.broadcasted_iota(I32, (128, 1), 0)
    sl = lax.broadcasted_iota(I32, (128, 128), 1)
    swap = (sl == lax.rem(sr // 2, 8) * 16 + sr // 16 * 2 + lax.rem(sr, 2)).astype(F32).astype(BF16)
    other = jnp.concatenate([mm(swap, hit[0:128]), mm(swap, hit[128:256])], axis=0).astype(BF16)
    tb[0:128, :] = mm(hit[0:128], sg[:, 0:512]).astype(BF16)
    tb[128:256, :] = mm(other[0:128], sg[:, 512:]).astype(BF16)
    g_core = put(tb, tr, 1, at(dc=1))
    g_core.start()
    ua[0:128, :] = mm(hit[128:256], sg[:, 0:512])
    ua[128:256, :] = mm(other[128:256], sg[:, 512:])

    for cp in large:
        cp.wait()
    ti = lax.broadcasted_iota(I32, (L, 1), 0)
    tj = lax.broadcasted_iota(I32, (L, L), 1)

    def shares(h):
        n = len_s[h]
        inv = 1.0 / jnp.full((1, 1), n, I32).astype(F32)
        return n, inv, jnp.where(ti < n, 1.0, 0.0) * inv

    def forward(h, carry):
        n, inv, keep = shares(h)
        xf = hist[h].astype(F32)
        r = lax.rsqrt(jnp.sum(xf * xf, axis=1, keepdims=True) * (1.0 / D) + 1e-05)
        rs[h] = jnp.broadcast_to(r, (L, HD))
        zz = mm((xf * r).astype(BF16), wi[...])
        sig = 1.0 / (1.0 + jnp.exp(-zz))
        p = zz * sig
        ds = sig + p * (1.0 - sig)
        dsl[h] = ds[:, 2 * HD :]
        pj[h] = p[:, HD:].astype(BF16)
        s = mm(pj[h, :, HD : 2 * HD], pj[h, :, 2 * HD :], NT) * HD**-0.5
        vis = (tj <= ti) & (tj < n)
        ss = 1.0 / (1.0 + jnp.exp(-s))
        sw = s * ss
        wgt[h] = (jnp.where(vis, sw, 0.0) * inv).astype(BF16)
        dsw[h] = jnp.where(vis, ss + sw * (1.0 - ss), 0.0) * (inv * HD**-0.5)
        att = mm(wgt[h], pj[h, :, 0:HD])
        mixed = (att * p[:, 0:HD]).astype(BF16).astype(F32)
        mvec[h] = jnp.broadcast_to(jnp.sum(mixed * keep, axis=0, keepdims=True), (8, HD))
        kg = keep * p[:, 0:HD]
        kgate[h] = kg
        pg = keep * att * ds[:, 0:HD]
        pv = mm(wgt[h], kg.astype(BF16), TN) * ds[:, HD : 2 * HD]
        pre[h, :, 0:HD] = pg
        pre[h, :, HD:] = pv
        preg[h, :, 0:HD] = (pg * r).astype(BF16)
        preg[h, :, HD:] = (pv * r).astype(BF16)
        return carry

    lax.fori_loop(0, 1, forward, 0)
    g_core.wait_recv()
    ua[...] = ua[...] + tr[...].astype(F32)
    ub[...] = ua[...].astype(BF16)
    many(ub, gzr, 3, "dz_", 16)
    many(ub.at[128:256], gzr.at[128:256], 15, "dy", 16)
    lax.fori_loop(1, 2, forward, 0)


    @pl.when(c == 1)
    def _():
        put(vzr.at[0:480], vzr.at[0:480], 0, at(dc=1)).wait_recv()
        s = tv[0:32, :]
        for k in range(15):
            s = s + vzr[32 * k : 32 * k + 32, :].astype(F32)
        for k in range(8):
            vys[0, k] = s[4 * k : 4 * k + 2]
            vys[1, k] = s[4 * k + 2 : 4 * k + 4]
        for k in RING:
            put(vys.at[0, k], vyr.at[k], 4, at(dy=k, core=0)).start()
            put(vys.at[1, k], vyr.at[k], 2, at(dy=k)).start()
        put(vys.at[0, 0], vyr.at[0], 4, at(dc=1)).start()
        vyr[0] = s[2:4]

    pr = lax.broadcasted_iota(I32, (512, 1), 0)
    fl = lax.broadcasted_iota(I32, (512, D), 1)

    def permute(i, carry):
        r = pr + i * 512
        crel, xrel, ry_, rz_, j = r // 512, lax.rem(r // 128, 4), lax.rem(r // 16, 8), lax.rem(r // 2, 8), lax.rem(r, 2)
        f = (lax.rem(y + ry_, 8) * 8 + lax.rem(z + rz_, 8)) * 2 + lax.rem(c + 1 - crel + 2, 2)
        f = f * 8 + lax.rem(x + xrel, 4) * 2 + j
        rows = pl.ds(pl.multiple_of(i * 512, 512), 512)
        pm = (fl == f).astype(F32).astype(BF16)
        pz[rows, :] = pm
        xz[rows, :] = mm(pm, hist[...].reshape(2 * L, D), NT).astype(BF16)
        for h in range(2):
            cpre[h, rows, :] = mm(xz[rows, h * L : (h + 1) * L], preg[h])
        return carry

    lax.fori_loop(0, 2, permute, 0)
    for k in range(0, D, 128):
        xq[k : k + 128, :] = mm(swap, xz[k : k + 128, :]).astype(BF16)

    whole(ub, gzr, 3, "dz_", 16).wait_recv()
    whole(ub.at[128:256], gzr.at[128:256], 15, "dy", 16).wait_recv()
    mine = []
    for p, i, axis in ((0, 5, "dy"), (1, 16, "dz_")):
        s1 = ua[128 * p : 128 * p + 16, :]
        for k in range(1, 8):
            s1 = s1 + gzr[128 * p + 16 * k : 128 * p + 16 * k + 16, :].astype(F32)
        mine.append(s1[0:2])
        s1 = s1.astype(BF16)
        for k in range(1, 8):
            gys[p, k] = s1[2 * k : 2 * k + 2]
        many(gys.at[p], gyr.at[p], i, axis)

    @pl.when(c == 1)
    def _():
        whole(vys.at[1], vyr, 2, "dy").wait_recv()

    @pl.when(c == 0)
    def _():
        put(vyr, vyr, 4, at(dc=1)).wait_recv()

    v = jnp.sum(vyr[...], axis=0)
    va = jnp.concatenate([v[0:1], v[0:1]], axis=1)
    vc = jnp.concatenate([v[1:2], v[1:2]], axis=1)
    cb[...] = (cpre[0, 0:512, :] * va + cpre[1, 0:512, :] * vc).astype(BF16)
    c1 = put(cb, cr, 6, at(dc=1))
    c1.start()
    for h in range(2):
        datt = (kgate[h] * v[h : h + 1, :]).astype(BF16)
        ds = (mm(datt, pj[h, :, 0:HD], NT) * dsw[h]).astype(BF16)
        dq = mm(ds, pj[h, :, 2 * HD :])
        dk = mm(ds, pj[h, :, HD : 2 * HD], TN)
        hr = slice(h * L, (h + 1) * L)
        for i, part in enumerate((dq, dk)):
            full = part * dsl[h, :, i * HD : (i + 1) * HD]
            dz[hr, (i + 2) * HD : (i + 3) * HD] = full.astype(BF16)
            dzr[hr, i * HD : (i + 1) * HD] = (full * rs[h]).astype(BF16)

    def regroup(r):
        return jnp.concatenate([r[a * 128 + b * 16 : a * 128 + b * 16 + 16] for b in range(8) for a in range(4)], axis=0)

    kc[0:512, :] = regroup(mm(xz[0:512, :], dzr[:, HD:])).astype(BF16)
    kc[512:1024, :] = regroup(mm(xq[0:512, :], dzr[:, 0:HD])).astype(BF16)
    c2 = put(kc, kcr, 7, at(dc=1))
    c2.start()
    own[...] = cpre[0, 512:1024, :] * va + cpre[1, 512:1024, :] * vc
    c1.wait_recv()
    for k in (2, 1, 3):
        a = slice(k * 128, (k + 1) * 128)
        xb[k] = (own[a, :] + cr[a, :].astype(F32)).astype(BF16)
        put(xb.at[k], xr.at[k], 8, at(dx=k)).start()
    kown[0:512, :] = regroup(mm(xz[512:1024, :], dzr[:, HD:]))
    kown[512:1024, :] = regroup(mm(xq[512:1024, :], dzr[:, 0:HD]))
    c2.wait_recv()
    for k in RING:
        for p, i, axis in ((0, 9, "dy"), (1, 12, "dz_")):
            a = slice(p * 512 + k * 64, p * 512 + k * 64 + 64)
            kb[p, k] = (kown[a, :] + kcr[a, :].astype(F32)).astype(BF16)
            put(kb.at[p, k], kr.at[p, k], i, at(**{axis: k})).start()

    whole(gys.at[0], gyr.at[0], 5, "dy").wait_recv()
    whole(gys.at[1], gyr.at[1], 16, "dz_").wait_recv()
    g = jnp.concatenate([mine[p] + jnp.sum(gyr[p, 1:8].astype(F32), axis=0) for p in range(2)], axis=1)
    gp = mm(jnp.concatenate([g, jnp.zeros((6, D), F32)], axis=0).astype(BF16), pz[...], NT)
    m2 = jnp.concatenate([mvec[0, 0:1, :], mvec[1, 0:1, :]], axis=0)
    for dc in range(2):
        for dx in range(4):
            q = (1 - dc) * 4 + dx
            gm[dc * 4 + dx, 0:2, :] = gp[0:2, q * HD : (q + 1) * HD]
            gm[dc * 4 + dx, 2:4, :] = m2
    for k in (6, 2, 5, 7, 1, 3, 4):
        put(gm.at[k], gmr.at[k], 10, at(dc=k // 4, dx=k % 4)).start()
    gmr[0] = gm[0]

    def back(h, carry):
        n, inv, keep = shares(h)
        hr = pl.ds(pl.multiple_of(h * L, L), L)
        vh = jnp.where(h == 0, va, vc)
        dz[hr, 0 : 2 * HD] = (pre[h] * vh).astype(BF16)
        dn = mm(dz[hr, :], wi[...], NT)
        r = rs[h, :, 0:1]
        xn = hist[h].astype(F32) * r
        mean = jnp.sum(dn * xn, axis=1, keepdims=True) * (1.0 / D)
        gh = jnp.where(h == 0, g[0:1, :], g[1:2, :])
        dx_o[h] = (r * (dn - xn * mean) + keep * gh).astype(BF16)
        return carry


    whole(xb, xr, 8, "dx").wait_recv()
    t0 = own[0:128, :] + cr[0:128, :].astype(F32)
    for k in range(1, 4):
        t0 = t0 + xr[k].astype(F32)
    put(gm.at[1:8], gmr.at[1:8], 10, at(dc=1)).wait_recv()
    gx = jnp.concatenate([gmr[k, 0:2, :] for k in range(8)], axis=0)
    mx = jnp.concatenate([gmr[k, 2:4, :] for k in range(8)], axis=0)
    so = mm(gx.astype(BF16), mx.astype(BF16), TN)
    t = jnp.concatenate([t0, so], axis=1)
    fbt[...] = t.astype(BF16)
    for a in RING + (0,):
        for b in RING + (0,):
            k = a * 8 + b
            if k:
                fb[k] = fbt[2 * k : 2 * k + 2, :]
                put(fb.at[k], fr.at[k], 11, at(dy=a, dz_=b)).start()


    tk = []
    for p, i, axis in ((0, 9, "dy"), (1, 12, "dz_")):
        whole(kb.at[p], kr.at[p], i, axis).wait_recv()
        a = slice(p * 512, p * 512 + 64)
        q = kown[a, :] + kcr[a, :].astype(F32)
        for k in range(1, 8):
            q = q + kr[p, k].astype(F32)
        tk.append(q[0:2])
        for a in (2, 1, 3, 0):
            for b in RING + (0,):
                k = a * 8 + b
                if k:
                    kf[p, k] = q[2 * k : 2 * k + 2]
                    other = {"dx": a, ("dy", "dz_")[1 - p]: b}
                    put(kf.at[p, k], kfr.at[p, k], 13 + p, at(**other)).start()

    lax.fori_loop(0, 2, back, 0)

    @pl.when(c == 0)
    def _():
        put(tvb, tvb, 0, at(dc=1)).wait_send()

    @pl.when(c == 1)
    def _():
        put(tvb.at[32:256], tvb.at[32:256], 0, at(dc=1)).wait_send()
        whole(vys.at[1], vyr, 2, "dy").wait_send()
        put(vys.at[0], vyr, 4, at(dc=1)).wait_send()

    for cp in (g_core, c1, c2):
        cp.wait_send()
    whole(ub, gzr, 3, "dz_", 16).wait_send()
    whole(ub.at[128:256], gzr.at[128:256], 15, "dy", 16).wait_send()
    whole(gys.at[0], gyr.at[0], 5, "dy").wait_send()
    whole(gys.at[1], gyr.at[1], 16, "dz_").wait_send()
    whole(xb, xr, 8, "dx").wait_send()
    whole(kb.at[0], kr.at[0], 9, "dy").wait_send()
    whole(kb.at[1], kr.at[1], 12, "dz_").wait_send()
    put(gm.at[1:8], gmr.at[1:8], 10, at(dc=1)).wait_send()

    put(fb.at[1:64], fr.at[1:64], 11, at(dy=1)).wait()
    f = t[0:2, :] + jnp.sum(fr[1:64].astype(F32), axis=0)
    gin_o[:, 0:256] = f[:, 0:256]
    gout_o[...] = f[:, 256:384]
    for p, cols in ((1, slice(256, 384)), (0, slice(384, 512))):
        put(kf.at[p, 1:32], kfr.at[p, 1:32], 13 + p, at(dx=1)).wait()
        gin_o[:, cols] = tk[p] + jnp.sum(kfr[p, 1:32], axis=0)


def finish(dx_v, gin_v, gout_v, dx_o, gin_o, gout_o, sem):
    pairs = [(dx_v.at[h, r : r + 128], dx_o.at[h, r : r + 128]) for h in range(2) for r in (0, 128)]
    pairs += [(gin_v, gin_o), (gout_v, gout_o)]
    copies = [pltpu.make_async_copy(a, b, sem.at[i]) for i, (a, b) in enumerate(pairs)]
    for copy in copies:
        copy.start()
    for copy in copies:
        copy.wait()


def body(sample_grads, send_count, send_user, histories, hist_len, w_in, w_out):
    vm = pl.BlockSpec(memory_space=pltpu.VMEM)
    hbm = pl.BlockSpec(memory_space=pl.ANY)
    V = pltpu.VMEM
    sd = jax.ShapeDtypeStruct
    dx, gin, gout = pl.pallas_call(
        kernel,
        out_shape=(V((2, L, D), BF16), V((2, 512), F32), V((2, HD), F32)),
        in_specs=[pl.BlockSpec(memory_space=pltpu.SMEM), hbm, hbm, hbm, hbm, hbm, hbm],
        out_specs=(vm, vm, vm),
        scratch_shapes=[
            V((1, 128), I32), V((4, 128), I32), V((256, D), BF16), V((2, L, D), BF16), V((D, 512), BF16), V((HD, D), BF16),
            V((256, HD), F32), V((256, HD), BF16), V((480, HD), BF16), V((2, 8, 2, HD), F32), V((8, 2, HD), F32),
            V((256, 512), BF16), V((256, 512), BF16), V((256, 512), F32), V((256, 512), BF16), V((256, 512), BF16),
            V((2, 8, 2, 512), BF16), V((2, 8, 2, 512), BF16),
            V((D, D), BF16), V((D, 512), BF16), V((D, 512), BF16),
            V((2, L, HD), F32), V((2, L, 256), F32), V((2, L, 256), BF16), V((2, L, L), BF16), V((2, L, L), F32),
            V((2, L, 3 * HD), BF16), V((2, L, 256), F32), V((2, L, HD), F32),
            V((512, 512), BF16), V((512, 256), BF16), V((2, 8, HD), F32), V((2, D, 256), F32),
            V((512, 256), BF16), V((512, 256), BF16), V((512, 256), F32),
            V((1024, HD), BF16), V((1024, HD), BF16), V((1024, HD), F32),
            V((4, 128, 256), BF16), V((4, 128, 256), BF16), V((2, 8, 64, HD), BF16), V((2, 8, 64, HD), BF16),
            V((8, 4, HD), F32), V((8, 4, HD), F32), V((128, 384), BF16), V((64, 2, 384), BF16), V((64, 2, 384), BF16),
            V((2, 32, 2, HD), F32), V((2, 32, 2, HD), F32),
            pltpu.SemaphoreType.DMA((6,)), pltpu.SemaphoreType.DMA((17,)), pltpu.SemaphoreType.DMA((17,)),
        ],
        compiler_params=pltpu.CompilerParams(
            collective_id=0, has_side_effects=True, vmem_limit_bytes=VMEM
        ),
        name="encoder_backward",
    )(hist_len, send_count, send_user.T, sample_grads, histories, w_in, w_out)
    dx, gin, gout = pl.pallas_call(
        finish,
        out_shape=(sd((2, L, D), BF16), sd((2, 512), F32), sd((2, HD), F32)),
        in_specs=[vm, vm, vm],
        out_specs=(hbm, hbm, hbm),
        scratch_shapes=[pltpu.SemaphoreType.DMA((6,))],
        compiler_params=pltpu.CompilerParams(vmem_limit_bytes=8 * 1024 * 1024),
        name="finish",
    )(dx, gin, gout)
    return dx, gin, gout.T


def solution(mesh):
    both = ("own", "rep")
    return jax.shard_map(
        body,
        mesh=mesh,
        in_specs=(P(both, None), P(both, None), P(both, None), P(both, None, None), P(both), P(), P()),
        out_specs=(P(both, None, None), P(both, None), P(None, both)),
        check_vma=False,
    )
```
